32 devices in a mesh: grp: 2 (over y), band: 4 (over z), strm: 4 (over x, core).
Axes of the slice: x: 2, y: 2, z: 4, core: 2. Of those that a mesh axis runs over, the one named last changes fastest.
Arguments:
- latents: bfloat16 [8, 2, 4, 16, 384], P(('grp', 'strm'), None, 'band'), parts along dimension 0, may hold values from -6 to 6
- cache_first: bfloat16 [8, 2, 4, 16, 384], P(('grp', 'strm'), None, 'band'), parts along dimension 0, may hold values from -6 to 6
- cache_second: bfloat16 [8, 2, 8, 32, 192], P(('grp', 'strm'), None, 'band'), parts along dimension 0, may hold values from -6 to 6
- gain_first: float32 [384], replicated, may hold values from 0.25 to 1.75
- gain_second: float32 [192], replicated, may hold values from 0.25 to 1.75
- w_first: bfloat16 [3, 3, 3, 384, 768], P(None, None, None, None, 'strm'), may hold values from -0.0625 to 0.0625
- w_second: bfloat16 [3, 3, 3, 192, 192], P(None, None, None, None, 'strm'), may hold values from -0.078125 to 0.078125
- cache_slot: int32 [8], P('grp'), parts along dimension 0, may hold values from 0 to 3, as said below
- block_index: int32 [8], P('grp'), parts along dimension 0, may hold values from 0 to 3, as said below
Outputs:
- decoded: bfloat16 [8, 2, 8, 32, 192], P(('grp', 'strm'), None, 'band'), parts along dimension 0
The draws below stay inside these ranges and needn't reach their ends.
There are 2 independent parts, one for each index of `grp`. The reference program is written for one: setup_inputs(seed, part) draws one part's arguments, and reference() takes and returns one part's arrays. A program takes and returns all parts, laid end to end along the dimension named above; an argument that names none is the same for every part. Nothing has to cross between parts.
Inputs may be any that keep to these rules, and one draw needn't show every extreme that they name: `cache_slot`: each slot holds the caches of exactly one stream. The caches are read only where block_index > 0; exactly one stream of a group has block number 0.
All inputs are finite; a program needn't handle non-finite values.
Results may differ from the reference program's by a relative error of at most 0.0056.
Values may be sent and summed in bfloat16 or wider, within the bound.
No kernel may reach another device: no remote copies, remote signals or barrier semaphores. Data moves between devices by JAX's collectives and lax.ppermute only.
A program may use at most 64 MiB of HBM per device.

```python
import jax
import jax.numpy as jnp
from jax import lax

C_IN = 384
C_OUT = 192
FRAMES = 2
COLS = 16
STREAMS = 4
HEIGHT = 4


def draw_cache_slot(key, part):
    return jax.random.permutation(jax.random.fold_in(key, 11), STREAMS).astype(jnp.int32)


def draw_block_index(key, part):
    inner = jax.random.fold_in(key, 23)
    values = jax.random.randint(jax.random.fold_in(inner, 1), (STREAMS,), 1, 4).astype(jnp.int32)
    fresh = jax.random.randint(jax.random.fold_in(inner, 2), (), 0, STREAMS).astype(jnp.int32)
    positions = jnp.arange(STREAMS, dtype=jnp.int32)
    return jnp.where(positions == fresh, jnp.zeros_like(values), values).astype(jnp.int32)


def block_scale(key, extent, split, least, largest):
    factor_of, own = 1.0, jax.random.fold_in(key, 6)
    for position, shards_of in split:
        steps = jnp.exp(jax.random.uniform(jax.random.fold_in(own, position), (shards_of,), jnp.float32, least / len(split), largest / len(split)))
        factor_of = factor_of * jnp.repeat(steps, extent[position] // shards_of).reshape([-1 if axis == position else 1 for axis in range(len(extent))])
    return factor_of


def gaussian(stream_key, shape, scale, bound, pieces=(), kind=jnp.bfloat16):
    factor_of = block_scale(stream_key, shape, pieces, -0.22, 0.18) if pieces else 1.0
    drawn = jax.random.normal(stream_key, shape, jnp.float32) * scale * factor_of
    return jnp.minimum(jnp.maximum(drawn, -bound), bound).astype(kind)


def setup_inputs(seed: int = 0, part: int = 0) -> dict:
    arg_keys = jax.random.split(jax.random.key(seed), 10)
    own_keys = jax.random.split(jax.random.fold_in(arg_keys[9], part), 10)
    return {
        "latents": gaussian(own_keys[0], (STREAMS, FRAMES, HEIGHT, COLS, C_IN), 1.0, 6.0, ((0, 4), (2, 4))),
        "cache_first": gaussian(own_keys[1], (STREAMS, 2, HEIGHT, COLS, C_IN), 1.0, 6.0, ((0, 4), (2, 4))),
        "cache_second": gaussian(own_keys[2], (STREAMS, 2, 2 * HEIGHT, 2 * COLS, C_OUT), 1.0, 6.0, ((0, 4), (2, 4))),
        "gain_first": jnp.clip(1.0 + 0.15 * jax.random.normal(arg_keys[3], (C_IN,), jnp.float32), 0.25, 1.75),
        "gain_second": jnp.clip(1.0 + 0.15 * jax.random.normal(arg_keys[4], (C_OUT,), jnp.float32), 0.25, 1.75),
        "w_first": gaussian(arg_keys[5], (3, 3, 3, C_IN, 4 * C_OUT), (27 * C_IN) ** -0.5, 0.0625, ((4, 4),)),
        "w_second": gaussian(arg_keys[6], (3, 3, 3, C_OUT, C_OUT), (27 * C_OUT) ** -0.5, 0.078125, ((4, 4),)),
        "cache_slot": draw_cache_slot(jax.random.fold_in(jax.random.fold_in(arg_keys[9], part), 71), part),
        "block_index": draw_block_index(jax.random.fold_in(jax.random.fold_in(arg_keys[9], part), 71), part),
    }


epsilon = 1e-06

def norm_silu(values, gain):
    mean_square = lax.optimization_barrier(jnp.mean(values * values, axis=-1, keepdims=True))
    return jax.nn.silu(values * lax.rsqrt(mean_square + epsilon) * gain.astype(jnp.float32))

def causal_conv(inputs, weight):
    padded = jnp.pad(inputs, ((0, 0), (0, 0), (0, 0), (1, 1), (0, 0)))
    count, span, height, width, channels = padded.shape
    frames = span - 2
    rows = height - 2
    columns = width - 2
    outputs = weight.shape[-1]
    summed = jnp.zeros((count * frames * rows * columns, outputs), jnp.float32)
    for frame_tap in range(3):
        for row_tap in range(3):
            window = padded[:, frame_tap:frame_tap + frames, row_tap:row_tap + rows]
            stacked = jnp.concatenate([window[:, :, :, col_tap:col_tap + columns] for col_tap in range(3)], axis=-1)
            kernel = weight[frame_tap, row_tap].reshape(3 * channels, outputs)
            summed = summed + jnp.dot(stacked.reshape(-1, 3 * channels), kernel, preferred_element_type=jnp.float32)
    return summed.reshape(count, frames, rows, columns, outputs)

def earlier_frames(slot_cache, slots, keep_mask):
    chosen = jnp.take(slot_cache, slots, axis=0)
    return jnp.where(keep_mask[:, None, None, None, None], chosen, jnp.zeros_like(chosen))

def to_space(values):
    count, frames, rows, columns, channels = values.shape
    quarter = channels // 4
    spread = values.reshape(count, frames, rows, columns, 2, 2, quarter)
    spread = spread.transpose(0, 1, 2, 4, 3, 5, 6)
    return spread.reshape(count, frames, 2 * rows, 2 * columns, quarter)

def reference(latents, cache_first, cache_second, gain_first, gain_second, w_first, w_second, cache_slot, block_index):
    keep_mask = block_index > 0
    first_act = norm_silu(latents.astype(jnp.float32), gain_first).astype(jnp.bfloat16)
    frames = jnp.concatenate([earlier_frames(cache_first, cache_slot, keep_mask), first_act], axis=1)
    frames = jnp.pad(frames, ((0, 0), (0, 0), (1, 1), (0, 0), (0, 0)))
    first_conv = causal_conv(frames, w_first).astype(jnp.bfloat16)
    upsampled = to_space(first_conv)
    second_act = norm_silu(upsampled.astype(jnp.float32), gain_second).astype(jnp.bfloat16)
    second = jnp.concatenate([earlier_frames(cache_second, cache_slot, keep_mask), second_act], axis=1)
    second = jnp.pad(second, ((0, 0), (0, 0), (1, 1), (0, 0), (0, 0)))
    branch = causal_conv(second, w_second).astype(jnp.bfloat16)
    return (upsampled.astype(jnp.float32) + branch.astype(jnp.float32)).astype(jnp.bfloat16)
```

```python
import functools

import jax
import jax.numpy as jnp
from jax import lax
from jax.experimental import pallas as pl
from jax.experimental.pallas import tpu as pltpu
from jax.sharding import PartitionSpec as P

epsilon = 1e-06
f32 = jnp.float32
bf16 = jnp.bfloat16


def norm_silu(values, gain):
    mean_square = jnp.mean(values * values, axis=-1, keepdims=True)
    return jax.nn.silu(values * lax.rsqrt(mean_square + epsilon) * gain)


def dot(lhs, rhs, transposed=False):
    dims = (((1,), (1,)), ((), ())) if transposed else (((1,), (0,)), ((), ()))
    return lax.dot_general(lhs, rhs, dims, preferred_element_type=f32)


def shifted(values, width):
    count = values.shape[0]
    place = lax.broadcasted_iota(jnp.int32, values.shape, 0) % width
    left = jnp.where(place == 0, 0.0, pltpu.roll(values, 1, 0))
    right = jnp.where(place == width - 1, 0.0, pltpu.roll(values, count - 1, 0))
    return left, values, right


def first_kernel(frames, columns, meta, *refs):
    latents, firsts, seconds = refs[0:4], refs[4:8], refs[8:12]
    gain, weight = refs[12:14]
    far, near, two, own, mid = refs[14:19]
    slot_first, slot_second = refs[19:21]
    me = meta[8]
    upper = me // 2 == 0
    channels = latents[0].shape[-1]
    outputs = weight.shape[-2]
    for d in range(4):
        slot_first[me ^ d] = firsts[d][...].reshape(2, columns, channels)
        slot_second[me ^ d] = seconds[d][0]

    parts = []
    for d in range(4):
        stream = me ^ d
        chosen = slot_first[meta[stream]].astype(f32)
        chosen = jnp.where(meta[4 + stream] > 0, chosen, 0.0)
        fresh = latents[d][...].reshape(frames * columns, channels).astype(f32)
        parts += [chosen.reshape(2 * columns, channels), norm_silu(fresh, gain[...])]
    views = [
        view.astype(bf16).reshape(4, frames + 2, columns, channels)
        for view in shifted(jnp.concatenate(parts, axis=0), columns)
    ]
    rows = 4 * frames * columns
    sums = [jnp.zeros((rows, outputs), f32) for _ in range(3)]
    taps = [jnp.where(upper, 2, 0), 1, jnp.where(upper, 0, 2)]
    for i in range(3):
        for l in range(3):
            window = views[l][:, i : i + frames].reshape(rows, channels)
            for j in range(3):
                sums[j] = sums[j] + dot(window, weight[i, taps[j], l], True)

    half = rows // 4

    def paired(values):
        return [
            jnp.concatenate([values[2 * p * half : (2 * p + 1) * half], values[(2 * p + 1) * half : (2 * p + 2) * half]], axis=1)
            for p in range(2)
        ]

    u, v, w = paired(sums[0]), paired(sums[1]), paired(sums[2])
    for p in range(2):
        at = pl.ds(p * half, half)
        after = pl.ds((2 + p) * half, half)
        far[at, :] = u[p].astype(bf16)
        far[after, :] = v[p].astype(bf16)
        two[at, :] = u[p].astype(bf16)
        near[at, :] = w[p].astype(bf16)
        own[at, :] = v[p]
        own[after, :] = w[p]

    chosen = slot_second[meta[me]].astype(f32)
    chosen = jnp.where(meta[4 + me] > 0, chosen, 0.0)
    mid[...] = chosen.astype(bf16)
    edges = [jnp.concatenate([chosen[0, r], chosen[1, r]], axis=-1) for r in range(2)]
    width = 2 * columns
    far[pl.ds(4 * half, width), :] = jnp.where(upper, edges[0], edges[1]).astype(bf16)
    near[pl.ds(2 * half, width), :] = jnp.where(upper, edges[1], edges[0]).astype(bf16)


def sum_kernel(half, meta, own, far, near, two, first_pair, second_pair):
    me, place, bands = meta[8], meta[9], meta[10]
    outside = jnp.where(me // 2 == 0, place == bands - 1, place == 0)
    for p, pair in enumerate((first_pair, second_pair)):
        at = pl.ds(p * half, half)
        after = pl.ds((2 + p) * half, half)
        centre = own[at, :] + far[at, :].astype(f32) + near[at, :].astype(f32)
        extra = own[after, :] + far[after, :].astype(f32) + two[at, :].astype(f32)
        pair[pl.ds(0, half), :] = centre.astype(bf16)
        pair[pl.ds(half, half), :] = jnp.where(outside, 0.0, extra).astype(bf16)


def second_kernel(frames, columns, meta, *refs):
    pairs, mid, far, near = refs[0:4], refs[4], refs[5], refs[6]
    weights, gain, out = refs[7:11], refs[11], refs[12]
    taps, quarters, sems = refs[13:16]
    me = meta[8]
    upper = me // 2 == 0
    channels = out.shape[-1]
    group = channels // 4
    half = frames * columns
    width = 2 * columns
    copies = [
        pltpu.make_async_copy(
            weights[d], taps.at[:, :, :, pl.ds(pl.multiple_of((me ^ d) * group, 16), group), :], sems.at[d]
        )
        for d in range(4)
    ]
    for copy in copies:
        copy.start()

    for e in range(4):
        quarters[me ^ e] = pairs[e][:, (e % 2) * channels : (e % 2 + 1) * channels]

    fields = [quarters[q].astype(f32).reshape(2, frames, columns, channels) for q in range(4)]
    row_of = ((1, 1), (0, 0), (1, 0), (0, 1))
    upsampled = jnp.stack(
        [jnp.stack([jnp.stack([fields[2 * a + b][c, t] for b in range(2)]) for a, c in row_of]) for t in range(frames)]
    )
    act = norm_silu(upsampled.reshape(-1, channels), gain[...])
    left, same, right = [
        v.astype(bf16).reshape(frames, 4, 2, columns, channels) for v in shifted(act, columns)
    ]

    def split(first, second):
        return jnp.stack([first, second], axis=2)

    act_views = [
        split(left[:, :, 1], same[:, :, 0]),
        same,
        split(same[:, :, 1], right[:, :, 0]),
    ]

    beyond = far[pl.ds(4 * half, width), :]
    behind = near[pl.ds(2 * half, width), :]
    top = jnp.where(upper, behind.astype(f32), beyond.astype(f32)).astype(bf16)
    bottom = jnp.where(upper, beyond.astype(f32), behind.astype(f32)).astype(bf16)
    stored = jnp.stack(
        [
            jnp.stack([top[:, f * channels : (f + 1) * channels], mid[f, 0], mid[f, 1], bottom[:, f * channels : (f + 1) * channels]])
            for f in range(2)
        ]
    ).reshape(2 * 4 * width, channels)
    size = stored.shape[0]
    row = lax.broadcasted_iota(jnp.int32, (size, size), 0)
    column = lax.broadcasted_iota(jnp.int32, (size, size), 1)
    inside = row % width
    natural = 2 * (inside % columns) + inside // columns
    cache_views = []
    for l in range(3):
        source = natural + (l - 1)
        keep = (source >= 0) & (source < width) & (column == row - inside + source)
        pick = jnp.where(keep, 1.0, 0.0).astype(bf16)
        cache_views.append(dot(pick, stored).astype(bf16).reshape(2, 4, 2, columns, channels))

    for copy in copies:
        copy.wait()

    area = 2 * width
    early = jnp.zeros((area, channels), f32)
    late = jnp.zeros((area, channels), f32)
    for j in range(3):
        for l in range(3):
            c0, c1 = [cache_views[l][f, j : j + 2].reshape(area, channels) for f in range(2)]
            a0, a1 = [act_views[l][f, j : j + 2].reshape(area, channels) for f in range(2)]
            early = early + dot(c0, taps[0, j, l], True) + dot(c1, taps[1, j, l], True) + dot(a0, taps[2, j, l], True)
            late = late + dot(c1, taps[0, j, l], True) + dot(a0, taps[1, j, l], True) + dot(a1, taps[2, j, l], True)

    row = lax.broadcasted_iota(jnp.int32, (area, area), 0)
    column = lax.broadcasted_iota(jnp.int32, (area, area), 1)
    inside = row % width
    keep = column == row - inside + (inside % 2) * columns + inside // 2
    order = jnp.where(keep, 1.0, 0.0).astype(bf16)
    for t, branch in enumerate((early, late)):
        base = upsampled[t, 1:3].reshape(area, channels)
        decoded = (base + branch.astype(bf16).astype(f32)).astype(bf16)
        out[0, t] = dot(order, decoded).astype(bf16).reshape(2, width, channels)


def whole(count):
    return [pl.BlockSpec(memory_space=pltpu.VMEM)] * count


SMEM = pl.BlockSpec(memory_space=pltpu.SMEM)


def body(latents, cache_first, cache_second, gain_first, gain_second, w_first, w_second, cache_slot, block_index):
    frames, columns, channels = latents.shape[1], latents.shape[3], latents.shape[4]
    outputs = w_first.shape[-1]
    bands = lax.axis_size("band")
    streams = lax.axis_size("strm")
    assert streams == 4 and latents.shape[2] == 1 and frames == 2
    half = frames * columns
    width = 2 * columns
    me = lax.axis_index("strm")
    place = lax.axis_index("band")
    meta = jnp.concatenate([cache_slot, block_index, jnp.stack([me, place, jnp.int32(bands)]).astype(jnp.int32)])

    def swapped(value, distance):
        return lax.ppermute(value, "strm", [(i, i ^ distance) for i in range(streams)])

    def along(value, step):
        pairs = []
        for band in range(bands):
            for k in range(streams):
                target = band - step if k // 2 == 0 else band + step
                if 0 <= target < bands:
                    pairs.append((band * streams + k, target * streams + k))
        return lax.ppermute(value, ("band", "strm"), pairs)

    def everyone(value):
        across = swapped(value, 2)
        return [value, swapped(value, 1), across, swapped(across, 1)]

    turned_first = jnp.swapaxes(w_first, 3, 4)
    turned_second = jnp.swapaxes(w_second, 3, 4)
    args = everyone(latents) + everyone(cache_first) + everyone(cache_second)
    pair = jax.ShapeDtypeStruct((2 * half, 2 * outputs), bf16)
    far, near, two, own, mid = pl.pallas_call(
        functools.partial(first_kernel, frames, columns),
        out_shape=[
            jax.ShapeDtypeStruct((4 * half + width, 2 * outputs), bf16),
            jax.ShapeDtypeStruct((2 * half + width, 2 * outputs), bf16),
            pair,
            jax.ShapeDtypeStruct((4 * half, 2 * outputs), f32),
            jax.ShapeDtypeStruct(cache_second.shape[1:], bf16),
        ],
        in_specs=[SMEM] + whole(14),
        out_specs=whole(5),
        scratch_shapes=[
            pltpu.VMEM((4,) + (2, columns, channels), bf16),
            pltpu.VMEM((4,) + cache_second.shape[1:], bf16),
        ],
        compiler_params=pltpu.CompilerParams(vmem_limit_bytes=24 * 2**20),
        name="first_conv",
    )(meta, *args, gain_first.reshape(1, -1), turned_first)
    weights = everyone(turned_second)
    far, near, two = along(far, 1), along(near, -1), along(two, 2)
    first_pair, second_pair = pl.pallas_call(
        functools.partial(sum_kernel, half),
        out_shape=[pair, pair],
        in_specs=[SMEM] + whole(4),
        out_specs=whole(2),
        name="row_sums",
    )(meta, own, far, near, two)
    across = swapped(second_pair, 2)
    pairs = [first_pair, swapped(first_pair, 1), across, swapped(across, 1)]
    decoded = pl.pallas_call(
        functools.partial(second_kernel, frames, columns),
        out_shape=jax.ShapeDtypeStruct((1, frames, 2, width, outputs), bf16),
        in_specs=[SMEM] + whole(7) + [pl.BlockSpec(memory_space=pl.ANY)] * 4 + whole(1),
        out_specs=pl.BlockSpec(memory_space=pltpu.VMEM),
        scratch_shapes=[
            pltpu.VMEM((3, 3, 3, outputs, outputs), bf16),
            pltpu.VMEM((4, 2 * half, outputs), bf16),
            pltpu.SemaphoreType.DMA((4,)),
        ],
        compiler_params=pltpu.CompilerParams(vmem_limit_bytes=24 * 2**20),
        name="second_conv",
    )(meta, *pairs, mid, far, near, *weights, gain_second.reshape(1, -1))
    return decoded


def solution(mesh):
    in_specs = (
        P(("grp", "strm"), None, "band", None, None),
        P(("grp", "strm"), None, "band", None, None),
        P(("grp", "strm"), None, "band", None, None),
        P(),
        P(),
        P(None, None, None, None, "strm"),
        P(None, None, None, None, "strm"),
        P("grp"),
        P("grp"),
    )
    out_specs = P(("grp", "strm"), None, "band", None, None)
    return jax.shard_map(body, mesh=mesh, in_specs=in_specs, out_specs=out_specs, check_vma=False)
```

```python
import functools

import jax
import jax.numpy as jnp
from jax import lax
from jax.experimental import pallas as pl
from jax.experimental.pallas import tpu as pltpu
from jax.sharding import PartitionSpec as P

epsilon = 1e-06
f32 = jnp.float32
bf16 = jnp.bfloat16


def norm_silu(values, gain):
    mean_square = jnp.mean(values * values, axis=-1, keepdims=True)
    return jax.nn.silu(values * lax.rsqrt(mean_square + epsilon) * gain)


def dot(lhs, rhs, transposed=False):
    dims = (((1,), (1,)), ((), ())) if transposed else (((1,), (0,)), ((), ()))
    return lax.dot_general(lhs, rhs, dims, preferred_element_type=f32)


def shifted(values, width):
    count = values.shape[0]
    place = lax.broadcasted_iota(jnp.int32, values.shape, 0) % width
    left = jnp.where(place == 0, 0.0, pltpu.roll(values, 1, 0))
    right = jnp.where(place == width - 1, 0.0, pltpu.roll(values, count - 1, 0))
    return left, values, right


def first_kernel(frames, columns, *refs):
    latents, firsts, seconds = refs[0:4], refs[4:8], refs[8:12]
    gain_there, weight_there, slots_there, blocks_there = refs[12:16]
    far, near, two, own, mid = refs[16:21]
    slot_first, slot_second, latent_here, weight, gain, slots, blocks, sems = refs[21:29]
    me = lax.axis_index("strm")
    upper = me // 2 == 0
    channels = latents[0].shape[-1]
    outputs = weight.shape[-2]
    loads = [
        pltpu.make_async_copy(latents[0], latent_here, sems.at[0]),
        pltpu.make_async_copy(firsts[0].at[0, :, 0], slot_first.at[me], sems.at[1]),
        pltpu.make_async_copy(seconds[0].at[0], slot_second.at[me], sems.at[2]),
        pltpu.make_async_copy(gain_there, gain, sems.at[3]),
        pltpu.make_async_copy(slots_there, slots, sems.at[4]),
        pltpu.make_async_copy(blocks_there, blocks, sems.at[5]),
    ]
    for load in loads:
        load.start()
    weight_loads = [pltpu.make_async_copy(weight_there.at[i], weight.at[i], sems.at[6 + i]) for i in range(3)]
    for load in weight_loads:
        load.start()
    for d in range(1, 4):
        slot_first[me ^ d] = firsts[d][...].reshape(2, columns, channels)
        slot_second[me ^ d] = seconds[d][0]
    for load in loads:
        load.wait()

    parts = []
    for d in range(4):
        stream = me ^ d
        chosen = slot_first[slots[stream]].astype(f32)
        chosen = jnp.where(blocks[stream] > 0, chosen, 0.0)
        source = latents[d] if d else latent_here
        fresh = source[...].reshape(frames * columns, channels).astype(f32)
        parts += [chosen.reshape(2 * columns, channels), norm_silu(fresh, gain[...][None, :])]
    views = [
        view.astype(bf16).reshape(4, frames + 2, columns, channels)
        for view in shifted(jnp.concatenate(parts, axis=0), columns)
    ]
    rows = 4 * frames * columns
    sums = [jnp.zeros((rows, outputs), f32) for _ in range(3)]
    taps = [jnp.where(upper, 2, 0), 1, jnp.where(upper, 0, 2)]
    for i in range(3):
        weight_loads[i].wait()
        for l in range(3):
            window = views[l][:, i : i + frames].reshape(rows, channels)
            for j in range(3):
                sums[j] = sums[j] + dot(window, weight[i, taps[j], l], True)

    half = rows // 4

    def paired(values):
        return [
            jnp.concatenate([values[2 * p * half : (2 * p + 1) * half], values[(2 * p + 1) * half : (2 * p + 2) * half]], axis=1)
            for p in range(2)
        ]

    u, v, w = paired(sums[0]), paired(sums[1]), paired(sums[2])
    for p in range(2):
        at = pl.ds(p * half, half)
        after = pl.ds((2 + p) * half, half)
        far[at, :] = u[p].astype(bf16)
        far[after, :] = v[p].astype(bf16)
        two[at, :] = u[p].astype(bf16)
        near[at, :] = w[p].astype(bf16)
        own[at, :] = v[p]
        own[after, :] = w[p]

    chosen = slot_second[slots[me]].astype(f32)
    chosen = jnp.where(blocks[me] > 0, chosen, 0.0)
    mid[...] = chosen.astype(bf16)
    edges = [jnp.concatenate([chosen[0, r], chosen[1, r]], axis=-1) for r in range(2)]
    width = 2 * columns
    far[pl.ds(4 * half, width), :] = jnp.where(upper, edges[0], edges[1]).astype(bf16)
    near[pl.ds(2 * half, width), :] = jnp.where(upper, edges[1], edges[0]).astype(bf16)


def sum_kernel(half, own, far, near, two, first_pair, second_pair):
    me, place, bands = lax.axis_index("strm"), lax.axis_index("band"), lax.axis_size("band")
    outside = jnp.where(me // 2 == 0, place == bands - 1, place == 0)
    for p, pair in enumerate((first_pair, second_pair)):
        at = pl.ds(p * half, half)
        after = pl.ds((2 + p) * half, half)
        centre = own[at, :] + far[at, :].astype(f32) + near[at, :].astype(f32)
        extra = own[after, :] + far[after, :].astype(f32) + two[at, :].astype(f32)
        pair[pl.ds(0, half), :] = centre.astype(bf16)
        pair[pl.ds(half, half), :] = jnp.where(outside, 0.0, extra).astype(bf16)


def second_kernel(frames, columns, *refs):
    pairs, mid, far, near = refs[0:4], refs[4], refs[5], refs[6]
    weights, gain, out = refs[7:11], refs[11], refs[12]
    taps, quarters, sems = refs[13:16]
    me = lax.axis_index("strm")
    upper = me // 2 == 0
    channels = out.shape[-1]
    group = channels // 4
    half = frames * columns
    width = 2 * columns
    copies = [
        pltpu.make_async_copy(
            weights[d], taps.at[:, :, :, pl.ds(pl.multiple_of((me ^ d) * group, 16), group), :], sems.at[d]
        )
        for d in range(4)
    ]
    for copy in copies:
        copy.start()

    for e in range(4):
        quarters[me ^ e] = pairs[e][:, (e % 2) * channels : (e % 2 + 1) * channels]

    fields = [quarters[q].astype(f32).reshape(2, frames, columns, channels) for q in range(4)]
    row_of = ((1, 1), (0, 0), (1, 0), (0, 1))
    upsampled = jnp.stack(
        [jnp.stack([jnp.stack([fields[2 * a + b][c, t] for b in range(2)]) for a, c in row_of]) for t in range(frames)]
    )
    act = norm_silu(upsampled.reshape(-1, channels), gain[...][None, :])
    left, same, right = [
        v.astype(bf16).reshape(frames, 4, 2, columns, channels) for v in shifted(act, columns)
    ]

    def split(first, second):
        return jnp.stack([first, second], axis=2)

    act_views = [
        split(left[:, :, 1], same[:, :, 0]),
        same,
        split(same[:, :, 1], right[:, :, 0]),
    ]

    beyond = far[pl.ds(4 * half, width), :]
    behind = near[pl.ds(2 * half, width), :]
    top = jnp.where(upper, behind.astype(f32), beyond.astype(f32)).astype(bf16)
    bottom = jnp.where(upper, beyond.astype(f32), behind.astype(f32)).astype(bf16)
    stored = jnp.stack(
        [
            jnp.stack([top[:, f * channels : (f + 1) * channels], mid[f, 0], mid[f, 1], bottom[:, f * channels : (f + 1) * channels]])
            for f in range(2)
        ]
    ).reshape(2 * 4 * width, channels)
    size = stored.shape[0]
    row = lax.broadcasted_iota(jnp.int32, (size, size), 0)
    column = lax.broadcasted_iota(jnp.int32, (size, size), 1)
    inside = row % width
    natural = 2 * (inside % columns) + inside // columns
    cache_views = []
    for l in range(3):
        source = natural + (l - 1)
        keep = (source >= 0) & (source < width) & (column == row - inside + source)
        pick = jnp.where(keep, 1.0, 0.0).astype(bf16)
        cache_views.append(dot(pick, stored).astype(bf16).reshape(2, 4, 2, columns, channels))

    for copy in copies:
        copy.wait()

    area = 2 * width
    early = jnp.zeros((area, channels), f32)
    late = jnp.zeros((area, channels), f32)
    for j in range(3):
        for l in range(3):
            c0, c1 = [cache_views[l][f, j : j + 2].reshape(area, channels) for f in range(2)]
            a0, a1 = [act_views[l][f, j : j + 2].reshape(area, channels) for f in range(2)]
            early = early + dot(c0, taps[0, j, l], True) + dot(c1, taps[1, j, l], True) + dot(a0, taps[2, j, l], True)
            late = late + dot(c1, taps[0, j, l], True) + dot(a0, taps[1, j, l], True) + dot(a1, taps[2, j, l], True)

    row = lax.broadcasted_iota(jnp.int32, (area, area), 0)
    column = lax.broadcasted_iota(jnp.int32, (area, area), 1)
    inside = row % width
    keep = column == row - inside + (inside % 2) * columns + inside // 2
    order = jnp.where(keep, 1.0, 0.0).astype(bf16)
    for t, branch in enumerate((early, late)):
        base = upsampled[t, 1:3].reshape(area, channels)
        decoded = (base + branch.astype(bf16).astype(f32)).astype(bf16)
        out[0, t] = dot(order, decoded).astype(bf16).reshape(2, width, channels)


def whole(count):
    return [pl.BlockSpec(memory_space=pltpu.VMEM)] * count


THERE = pl.BlockSpec(memory_space=pltpu.HBM)


def there(value):
    return pltpu.with_memory_space_constraint(value, pltpu.HBM)


def body(latents, cache_first, cache_second, gain_first, gain_second, w_first, w_second, cache_slot, block_index):
    frames, columns, channels = latents.shape[1], latents.shape[3], latents.shape[4]
    outputs = w_first.shape[-1]
    bands = lax.axis_size("band")
    streams = lax.axis_size("strm")
    assert streams == 4 and latents.shape[2] == 1 and frames == 2
    half = frames * columns
    width = 2 * columns

    def swapped(value, distance):
        return lax.ppermute(value, "strm", [(i, i ^ distance) for i in range(streams)])

    def along(value, step):
        pairs = []
        for band in range(bands):
            for k in range(streams):
                target = band - step if k // 2 == 0 else band + step
                if 0 <= target < bands:
                    pairs.append((band * streams + k, target * streams + k))
        return lax.ppermute(value, ("band", "strm"), pairs)

    def everyone(value):
        across = swapped(value, 2)
        return [value, swapped(value, 1), across, swapped(across, 1)]

    turned_first = jnp.swapaxes(w_first, 3, 4)
    turned_second = jnp.swapaxes(w_second, 3, 4)
    firsts = everyone(cache_first)
    args = everyone(latents) + firsts + everyone(cache_second)
    turned_second, *_ = lax.optimization_barrier((turned_second, args[2], args[6], args[10]))
    weights = [turned_second, swapped(turned_second, 1), swapped(turned_second, 2)]
    pair = jax.ShapeDtypeStruct((2 * half, 2 * outputs), bf16)
    far, near, two, own, mid = pl.pallas_call(
        functools.partial(first_kernel, frames, columns),
        out_shape=[
            jax.ShapeDtypeStruct((4 * half + width, 2 * outputs), bf16),
            jax.ShapeDtypeStruct((2 * half + width, 2 * outputs), bf16),
            pair,
            jax.ShapeDtypeStruct((4 * half, 2 * outputs), f32),
            jax.ShapeDtypeStruct(cache_second.shape[1:], bf16),
        ],
        in_specs=([THERE] + whole(3)) * 3 + [THERE] * 4,
        out_specs=whole(5),
        scratch_shapes=[
            pltpu.VMEM((4,) + (2, columns, channels), bf16),
            pltpu.VMEM((4,) + cache_second.shape[1:], bf16),
            pltpu.VMEM(latents.shape, bf16),
            pltpu.VMEM(turned_first.shape, bf16),
            pltpu.VMEM(gain_first.shape, f32),
            pltpu.SMEM(cache_slot.shape, jnp.int32),
            pltpu.SMEM(block_index.shape, jnp.int32),
            pltpu.SemaphoreType.DMA((9,)),
        ],
        compiler_params=pltpu.CompilerParams(vmem_limit_bytes=24 * 2**20),
        name="first_conv",
    )(
        *[there(v) if n % 4 == 0 else v for n, v in enumerate(args)],
        there(gain_first),
        there(turned_first),
        there(cache_slot),
        there(block_index),
    )
    far, near, two = along(far, 1), along(near, -1), along(two, 2)
    first_pair, second_pair = pl.pallas_call(
        functools.partial(sum_kernel, half),
        out_shape=[pair, pair],
        in_specs=whole(4),
        out_specs=whole(2),
        compiler_params=pltpu.CompilerParams(vmem_limit_bytes=8 * 2**20),
        name="row_sums",
    )(own, far, near, two)
    second_pair, weight_across = lax.optimization_barrier((second_pair, weights[2]))
    weights.append(swapped(weight_across, 1))
    across = swapped(second_pair, 2)
    pairs = [first_pair, swapped(first_pair, 1), across, swapped(across, 1)]
    decoded = pl.pallas_call(
        functools.partial(second_kernel, frames, columns),
        out_shape=jax.ShapeDtypeStruct((1, frames, 2, width, outputs), bf16),
        in_specs=whole(7) + [pl.BlockSpec(memory_space=pl.ANY)] * 4 + whole(1),
        out_specs=pl.BlockSpec(memory_space=pltpu.VMEM),
        scratch_shapes=[
            pltpu.VMEM((3, 3, 3, outputs, outputs), bf16),
            pltpu.VMEM((4, 2 * half, outputs), bf16),
            pltpu.SemaphoreType.DMA((4,)),
        ],
        compiler_params=pltpu.CompilerParams(vmem_limit_bytes=24 * 2**20),
        name="second_conv",
    )(*pairs, mid, far, near, *weights, gain_second)
    return decoded


def solution(mesh):
    in_specs = (
        P(("grp", "strm"), None, "band", None, None),
        P(("grp", "strm"), None, "band", None, None),
        P(("grp", "strm"), None, "band", None, None),
        P(),
        P(),
        P(None, None, None, None, "strm"),
        P(None, None, None, None, "strm"),
        P("grp"),
        P("grp"),
    )
    out_specs = P(("grp", "strm"), None, "band", None, None)
    return jax.shard_map(body, mesh=mesh, in_specs=in_specs, out_specs=out_specs, check_vma=False)
```

```python
import functools

import jax
import jax.numpy as jnp
from jax import lax
from jax.experimental import pallas as pl
from jax.experimental.pallas import tpu as pltpu
from jax.sharding import PartitionSpec as P

epsilon = 1e-06
f32 = jnp.float32
bf16 = jnp.bfloat16


def norm_silu(values, gain):
    mean_square = jnp.mean(values * values, axis=-1, keepdims=True)
    return jax.nn.silu(values * lax.rsqrt(mean_square + epsilon) * gain)


def dot(lhs, rhs, transposed=False):
    dims = (((1,), (1,)), ((), ())) if transposed else (((1,), (0,)), ((), ()))
    return lax.dot_general(lhs, rhs, dims, preferred_element_type=f32)


def shifted(values, width):
    count = values.shape[0]
    place = lax.broadcasted_iota(jnp.int32, values.shape, 0) % width
    left = jnp.where(place == 0, 0.0, pltpu.roll(values, 1, 0))
    right = jnp.where(place == width - 1, 0.0, pltpu.roll(values, count - 1, 0))
    return left, values, right


def halves(values):
    count = values.shape[0] // 2
    return jnp.concatenate([values[:count], values[count:]], axis=1)


def pack_kernel(latents, first, second, gain_there, out, latent_here, first_here, second_here, gain, sems):
    loads = [
        pltpu.make_async_copy(*pair, sems.at[n])
        for n, pair in enumerate(((gain_there, gain), (latents, latent_here), (first, first_here), (second, second_here)))
    ]
    for load in loads:
        load.start()
    rows, channels = latent_here.shape[1] * latent_here.shape[3], latent_here.shape[-1]
    width = second_here.shape[3]
    for load in loads:
        load.wait()
    out[pl.ds(0, rows), :] = first_here[...].reshape(rows, channels)
    act = norm_silu(latent_here[...].reshape(rows, channels).astype(f32), gain[...][None, :])
    out[pl.ds(rows, rows), :] = act.astype(bf16)
    for r in range(2):
        out[pl.ds(2 * rows + r * width, width), :] = jnp.concatenate([second_here[0, f, r] for f in range(2)], axis=1)


def fetch_kernel(packed, first_there, second_there, first, second, second_here, sems):
    del packed
    loads = [
        pltpu.make_async_copy(second_there, second_here, sems.at[0]),
        pltpu.make_async_copy(first_there, first, sems.at[1]),
    ]
    for load in loads:
        load.start()
    loads[0].wait()
    taps, group, channels = 27, second_here.shape[-2], second_here.shape[-1]
    values = second_here[...].reshape(taps * group, channels)
    most = (taps + 1) // 2 * group
    rest = taps * group - most
    second[pl.ds(0, rest), :] = jnp.concatenate([values[:rest], values[most:]], axis=1)
    last = values[rest:most]
    second[pl.ds(rest, group), :] = jnp.concatenate([last, last], axis=1)
    loads[1].wait()


def first_kernel(frames, columns, *refs):
    packs, weight, slots_there, blocks_there = refs[0:4], refs[4], refs[5], refs[6]
    one, other, two, own, mid = refs[7:12]
    held, slots, blocks, sems = refs[12:16]
    loads = [
        pltpu.make_async_copy(slots_there, slots, sems.at[0]),
        pltpu.make_async_copy(blocks_there, blocks, sems.at[1]),
    ]
    for load in loads:
        load.start()
    me = lax.axis_index("strm")
    upper = me // 2 == 0
    channels = held.shape[-1]
    outputs = weight.shape[-2]
    half = frames * columns
    width = 2 * columns
    for d in range(4):
        held[me ^ d] = packs[d][...]
    for load in loads:
        load.wait()

    parts = []
    for d in range(4):
        stream = me ^ d
        chosen = held[slots[stream], pl.ds(0, half)].astype(f32)
        parts.append(jnp.where(blocks[stream] > 0, chosen, 0.0))
        parts.append(packs[d][pl.ds(half, half), :].astype(f32))
    views = [
        view.astype(bf16).reshape(4, frames + 2, columns, channels)
        for view in shifted(jnp.concatenate(parts, axis=0), columns)
    ]
    rows = 4 * half
    sums = [jnp.zeros((rows, outputs), f32) for _ in range(3)]
    taps = [jnp.where(upper, 2, 0), 1, jnp.where(upper, 0, 2)]
    for i in range(3):
        for l in range(3):
            window = views[l][:, i : i + frames].reshape(rows, channels)
            for j in range(3):
                sums[j] = sums[j] + dot(window, weight[i, taps[j], l], True)

    u, v, w = [[halves(values[: 2 * half]), halves(values[2 * half :])] for values in sums]
    far_first = sends_far_first()
    cached = held[slots[me], pl.ds(2 * half, 2 * width)].astype(f32)
    cached = jnp.where(blocks[me] > 0, cached, 0.0)
    mid[...] = cached.astype(bf16)
    edges = [cached[:width], cached[width:]]
    far = u + v + [jnp.where(upper, edges[0], edges[1])]
    near = w + [jnp.zeros_like(w[0])] * 2 + [jnp.where(upper, edges[1], edges[0])]
    for n in range(5):
        at = pl.ds(n * half, half)
        one[at, :] = jnp.where(far_first, far[n], near[n]).astype(bf16)
        other[at, :] = jnp.where(far_first, near[n], far[n]).astype(bf16)
    for p in range(2):
        two[pl.ds(p * half, half), :] = u[p].astype(bf16)
        own[pl.ds(p * half, half), :] = v[p]
        own[pl.ds((2 + p) * half, half), :] = w[p]


def sends_far_first():
    return (lax.axis_index("strm") // 2 == 0) == (lax.axis_index("band") % 2 == 1)


def far_comes_first():
    return (lax.axis_index("strm") // 2 == 0) == (lax.axis_index("band") % 2 == 0)


def at_end():
    place = lax.axis_index("band")
    return (place == 0) | (place == lax.axis_size("band") - 1)


def sum_kernel(half, own, one, other, two, first_pair, second_pair):
    me, place, bands = lax.axis_index("strm"), lax.axis_index("band"), lax.axis_size("band")
    upper = me // 2 == 0
    outside = jnp.where(upper, place == bands - 1, place == 0)
    beyond = jnp.where(upper, place >= bands - 2, place <= 1)
    far_first = far_comes_first()
    alone = at_end()
    for p, pair in enumerate((first_pair, second_pair)):
        at = pl.ds(p * half, half)
        after = pl.ds((2 + p) * half, half)
        centre = own[at, :] + one[at, :].astype(f32) + jnp.where(alone, 0.0, other[at, :].astype(f32))
        extra = jnp.where(far_first, one[after, :].astype(f32), jnp.where(alone, 0.0, other[after, :].astype(f32)))
        extra = own[after, :] + extra + jnp.where(beyond, 0.0, two[at, :].astype(f32))
        pair[pl.ds(0, half), :] = centre.astype(bf16)
        pair[pl.ds(half, half), :] = jnp.where(outside, 0.0, extra).astype(bf16)


def cache_kernel(columns, mid, one, other, w0, w1, w2, w3, sums, weights, first_taps):
    me = lax.axis_index("strm")
    upper = me // 2 == 0
    far_first = far_comes_first()
    channels = sums.shape[-1]
    group = channels // 4
    width = 2 * columns
    area = 2 * width
    for d, quarter in enumerate((w0, w1, w2, w3)):
        at = pl.ds(pl.multiple_of((me ^ d) * group, 16), group)
        values = quarter[...].reshape(14, group, 2 * channels)
        left, right = values[:, :, :channels], values[:13, :, channels:]
        first_taps[:, at, :] = left[:9]
        weights[pl.ds(0, 5), at, :] = left[9:]
        weights[pl.ds(5, 13), at, :] = right

    first_edge = one[pl.ds(4 * width, width), :].astype(f32)
    second_edge = jnp.where(at_end(), 0.0, other[pl.ds(4 * width, width), :].astype(f32))
    far = jnp.where(far_first, first_edge, second_edge)
    near = jnp.where(far_first, second_edge, first_edge)
    top = jnp.where(upper, near, far).astype(bf16)
    bottom = jnp.where(upper, far, near).astype(bf16)
    stored = jnp.concatenate([top, mid[...], bottom], axis=0)
    size = stored.shape[0]
    row = lax.broadcasted_iota(jnp.int32, (size, size), 0)
    column = lax.broadcasted_iota(jnp.int32, (size, size), 1)
    inside = row % width
    natural = 2 * (inside % columns) + inside // columns
    early = jnp.zeros((area, channels), f32)
    late = jnp.zeros((area, channels), f32)
    for l in range(3):
        source = natural + (l - 1)
        keep = (source >= 0) & (source < width) & (column == row - inside + source)
        view = dot(jnp.where(keep, 1.0, 0.0).astype(bf16), stored).astype(bf16)
        c0, c1 = view[:, :channels], view[:, channels:]
        for j in range(3):
            at = slice(j * width, j * width + area)
            tap = 3 * j + l
            early = early + dot(c0[at], first_taps[tap], True) + dot(c1[at], weights[tap], True)
            late = late + dot(c1[at], first_taps[tap], True)
    sums[0] = early
    sums[1] = late


def second_kernel(frames, columns, p0, p1, p2, p3, sums, weights, gain, out, quarters):
    me = lax.axis_index("strm")
    channels = out.shape[-1]
    width = 2 * columns
    for e, pair in enumerate((p0, p1, p2, p3)):
        quarters[me ^ e] = pair[:, (e % 2) * channels : (e % 2 + 1) * channels]

    fields = [quarters[q].astype(f32).reshape(2, frames, columns, channels) for q in range(4)]
    row_of = ((1, 1), (0, 0), (1, 0), (0, 1))
    upsampled = jnp.stack(
        [jnp.stack([jnp.stack([fields[2 * a + b][c, t] for b in range(2)]) for a, c in row_of]) for t in range(frames)]
    )
    act = norm_silu(upsampled.reshape(-1, channels), gain[...][None, :])
    left, same, right = [
        v.astype(bf16).reshape(frames, 4, 2, columns, channels) for v in shifted(act, columns)
    ]

    def split(first, second):
        return jnp.stack([first, second], axis=2)

    views = [
        split(left[:, :, 1], same[:, :, 0]),
        same,
        split(same[:, :, 1], right[:, :, 0]),
    ]
    area = 2 * width
    early, late = sums[0], sums[1]
    for j in range(3):
        for l in range(3):
            a0, a1 = [views[l][f, j : j + 2].reshape(area, channels) for f in range(2)]
            tap = 3 * j + l
            early = early + dot(a0, weights[9 + tap], True)
            late = late + dot(a0, weights[tap], True) + dot(a1, weights[9 + tap], True)

    row = lax.broadcasted_iota(jnp.int32, (area, area), 0)
    column = lax.broadcasted_iota(jnp.int32, (area, area), 1)
    inside = row % width
    keep = column == row - inside + (inside % 2) * columns + inside // 2
    order = jnp.where(keep, 1.0, 0.0).astype(bf16)
    for t, branch in enumerate((early, late)):
        base = upsampled[t, 1:3].reshape(area, channels)
        decoded = (base + branch.astype(bf16).astype(f32)).astype(bf16)
        out[0, t] = dot(order, decoded).astype(bf16).reshape(2, width, channels)


def whole(count):
    return [pl.BlockSpec(memory_space=pltpu.VMEM)] * count


THERE = pl.BlockSpec(memory_space=pltpu.HBM)


def there(value):
    return pltpu.with_memory_space_constraint(value, pltpu.HBM)


def call(kernel, name, megabytes, **settings):
    return pl.pallas_call(
        kernel, name=name, compiler_params=pltpu.CompilerParams(vmem_limit_bytes=megabytes * 2**20), **settings
    )


def struct(shape, dtype=bf16):
    return jax.ShapeDtypeStruct(shape, dtype)


def body(latents, cache_first, cache_second, gain_first, gain_second, w_first, w_second, cache_slot, block_index):
    frames, columns, channels = latents.shape[1], latents.shape[3], latents.shape[4]
    outputs = w_first.shape[-1]
    bands = lax.axis_size("band")
    streams = lax.axis_size("strm")
    assert streams == 4 and bands % 2 == 0 and latents.shape[2] == 1 and frames == 2
    half = frames * columns
    width = 2 * columns

    def swapped(value, distance):
        return lax.ppermute(value, "strm", [(i, i ^ distance) for i in range(streams)])

    def along(value, target):
        pairs = []
        for band in range(bands):
            for k in range(streams):
                to, there = target(band, k)
                if 0 <= to < bands:
                    pairs.append((band * streams + k, to * streams + there))
        return lax.ppermute(value, ("band", "strm"), pairs)

    def first_way(band, k):
        return band ^ 1, k

    def second_way(band, k):
        if band in (0, bands - 1):
            return band, k ^ 1
        return ((band + 1) ^ 1) - 1, k

    def third_way(band, k):
        if bands == 4:
            return band ^ 2, k
        return (band - 2 if k // 2 == 0 else band + 2), k

    turned_first = jnp.swapaxes(w_first, 3, 4)
    turned_second = jnp.swapaxes(w_second, 3, 4)
    group = turned_second.shape[3]
    packed = call(
        pack_kernel,
        "pack",
        4,
        out_shape=struct((2 * half + 2 * width, channels)),
        in_specs=[THERE] * 4,
        out_specs=whole(1)[0],
        scratch_shapes=[
            pltpu.VMEM(latents.shape, bf16),
            pltpu.VMEM(cache_first.shape, bf16),
            pltpu.VMEM(cache_second.shape, bf16),
            pltpu.VMEM(gain_first.shape, f32),
            pltpu.SemaphoreType.DMA((4,)),
        ],
    )(*map(there, (latents, cache_first, cache_second, gain_first)))
    across = swapped(packed, 2)
    weight_first, weight_own = call(
        fetch_kernel,
        "fetch",
        16,
        out_shape=[struct(turned_first.shape), struct((14 * group, 2 * outputs))],
        in_specs=whole(1) + [THERE] * 2,
        out_specs=whole(2),
        scratch_shapes=[pltpu.VMEM(turned_second.shape, bf16), pltpu.SemaphoreType.DMA((2,))],
    )(packed, there(turned_first), there(turned_second))
    weight_own, across = lax.optimization_barrier((weight_own, across))
    packs = [packed, swapped(packed, 1), across, swapped(across, 1)]
    weights = [weight_own, swapped(weight_own, 1), swapped(weight_own, 2)]
    pair = struct((2 * half, 2 * outputs))
    payload = struct((4 * half + width, 2 * outputs))
    one, other, two, own, mid = call(
        functools.partial(first_kernel, frames, columns),
        "first_conv",
        16,
        out_shape=[payload, payload, pair, struct((4 * half, 2 * outputs), f32), struct((2 * width, 2 * outputs))],
        in_specs=whole(5) + [THERE] * 2,
        out_specs=whole(5),
        scratch_shapes=[
            pltpu.VMEM((4,) + packed.shape, bf16),
            pltpu.SMEM(cache_slot.shape, jnp.int32),
            pltpu.SMEM(block_index.shape, jnp.int32),
            pltpu.SemaphoreType.DMA((2,)),
        ],
    )(*packs, weight_first, there(cache_slot), there(block_index))
    one, other, two = along(one, first_way), along(other, second_way), along(two, third_way)
    first_pair, second_pair = call(
        functools.partial(sum_kernel, half),
        "row_sums",
        4,
        out_shape=[pair, pair],
        in_specs=whole(4),
        out_specs=whole(2),
    )(own, one, other, two)
    weight_across, _ = lax.optimization_barrier((weights[2], first_pair))
    weights.append(swapped(weight_across, 1))
    across = swapped(second_pair, 2)
    sums, taps = call(
        functools.partial(cache_kernel, columns),
        "cached_conv",
        16,
        out_shape=[struct((2, 2 * width, outputs), f32), struct((18, outputs, outputs))],
        in_specs=whole(7),
        out_specs=whole(2),
        scratch_shapes=[pltpu.VMEM((9, outputs, outputs), bf16)],
    )(mid, one, other, *weights)
    across, sums = lax.optimization_barrier((across, sums))
    pairs = [first_pair, swapped(first_pair, 1), across, swapped(across, 1)]
    return call(
        functools.partial(second_kernel, frames, columns),
        "second_conv",
        16,
        out_shape=struct((1, frames, 2, width, outputs)),
        in_specs=whole(7),
        out_specs=whole(1)[0],
        scratch_shapes=[pltpu.VMEM((4, 2 * half, outputs), bf16)],
    )(*pairs, sums, taps, gain_second)


def solution(mesh):
    in_specs = (
        P(("grp", "strm"), None, "band", None, None),
        P(("grp", "strm"), None, "band", None, None),
        P(("grp", "strm"), None, "band", None, None),
        P(),
        P(),
        P(None, None, None, None, "strm"),
        P(None, None, None, None, "strm"),
        P("grp"),
        P("grp"),
    )
    out_specs = P(("grp", "strm"), None, "band", None, None)
    return jax.shard_map(body, mesh=mesh, in_specs=in_specs, out_specs=out_specs, check_vma=False)
```

```python
import functools

import jax
import jax.numpy as jnp
from jax import lax
from jax.experimental import pallas as pl
from jax.experimental.pallas import tpu as pltpu
from jax.sharding import PartitionSpec as P

epsilon = 1e-06
f32 = jnp.float32
bf16 = jnp.bfloat16


def norm_silu(values, gain):
    mean_square = jnp.mean(values * values, axis=-1, keepdims=True)
    return jax.nn.silu(values * lax.rsqrt(mean_square + epsilon) * gain)


def dot(lhs, rhs, transposed=False):
    dims = (((1,), (1,)), ((), ())) if transposed else (((1,), (0,)), ((), ()))
    return lax.dot_general(lhs, rhs, dims, preferred_element_type=f32)


def shifted(values, width):
    count = values.shape[0]
    place = lax.broadcasted_iota(jnp.int32, values.shape, 0) % width
    left = jnp.where(place == 0, 0.0, pltpu.roll(values, 1, 0))
    right = jnp.where(place == width - 1, 0.0, pltpu.roll(values, count - 1, 0))
    return left, values, right


def halves(values):
    count = values.shape[0] // 2
    return jnp.concatenate([values[:count], values[count:]], axis=1)


def pack_kernel(latents, first, second, gain_there, out, latent_here, first_here, second_here, gain, sems):
    loads = [
        pltpu.make_async_copy(*pair, sems.at[n])
        for n, pair in enumerate(((gain_there, gain), (latents, latent_here), (first, first_here), (second, second_here)))
    ]
    for load in loads:
        load.start()
    rows, channels = latent_here.shape[1] * latent_here.shape[3], latent_here.shape[-1]
    width = second_here.shape[3]
    for load in loads:
        load.wait()
    out[pl.ds(0, rows), :] = first_here[...].reshape(rows, channels)
    act = norm_silu(latent_here[...].reshape(rows, channels).astype(f32), gain[...][None, :])
    out[pl.ds(rows, rows), :] = act.astype(bf16)
    for r in range(2):
        out[pl.ds(2 * rows + r * width, width), :] = jnp.concatenate([second_here[0, f, r] for f in range(2)], axis=1)


def fetch_kernel(
    packed, first_there, second_there, slots_there, blocks_there, first, second, masks, second_here, slots, blocks, sems
):
    del packed
    loads = [
        pltpu.make_async_copy(second_there, second_here, sems.at[0]),
        pltpu.make_async_copy(slots_there, slots, sems.at[1]),
        pltpu.make_async_copy(blocks_there, blocks, sems.at[2]),
        pltpu.make_async_copy(first_there, first, sems.at[3]),
    ]
    for load in loads:
        load.start()
    for load in loads[:3]:
        load.wait()
    me = lax.axis_index("strm")
    for d in range(4):
        for e in range(4):
            chosen = (slots[me ^ d] == me ^ e) & (blocks[me ^ d] > 0)
            masks[d, e] = jnp.full(masks.shape[2:], jnp.where(chosen, 1.0, 0.0), f32)
    taps, group, channels = 27, second_here.shape[-2], second_here.shape[-1]
    values = second_here[...].reshape(taps * group, channels)
    most = (taps + 1) // 2 * group
    rest = taps * group - most
    second[pl.ds(0, rest), :] = jnp.concatenate([values[:rest], values[most:]], axis=1)
    last = values[rest:most]
    second[pl.ds(rest, group), :] = jnp.concatenate([last, last], axis=1)
    loads[3].wait()


def first_kernel(frames, columns, p0, p1, p2, p3, weight, masks, one, other, two, own, mid):
    packs = (p0, p1, p2, p3)
    upper = lax.axis_index("strm") // 2 == 0
    channels = p0.shape[-1]
    outputs = weight.shape[-2]
    half = frames * columns
    width = 2 * columns

    def chosen(d, at):
        return sum(jnp.where(masks[d, e] > 0.5, packs[e][at, :].astype(f32), 0.0) for e in range(4))

    parts = []
    for d in range(4):
        parts.append(chosen(d, pl.ds(0, half)))
        parts.append(packs[d][pl.ds(half, half), :].astype(f32))
    views = [
        view.astype(bf16).reshape(4, frames + 2, columns, channels)
        for view in shifted(jnp.concatenate(parts, axis=0), columns)
    ]
    rows = 4 * half
    sums = [jnp.zeros((rows, outputs), f32) for _ in range(3)]
    taps = [jnp.where(upper, 2, 0), 1, jnp.where(upper, 0, 2)]
    for i in range(3):
        for l in range(3):
            window = views[l][:, i : i + frames].reshape(rows, channels)
            for j in range(3):
                sums[j] = sums[j] + dot(window, weight[i, taps[j], l], True)

    u, v, w = [[halves(values[: 2 * half]), halves(values[2 * half :])] for values in sums]
    far_first = sends_far_first()
    cached = chosen(0, pl.ds(2 * half, 2 * width))
    mid[...] = cached.astype(bf16)
    edges = [cached[:width], cached[width:]]
    far = u + v + [jnp.where(upper, edges[0], edges[1])]
    near = w + [jnp.zeros_like(w[0])] * 2 + [jnp.where(upper, edges[1], edges[0])]
    for n in range(5):
        at = pl.ds(n * half, half)
        one[at, :] = jnp.where(far_first, far[n], near[n]).astype(bf16)
        other[at, :] = jnp.where(far_first, near[n], far[n]).astype(bf16)
    for p in range(2):
        two[pl.ds(p * half, half), :] = u[p].astype(bf16)
        own[pl.ds(p * half, half), :] = v[p]
        own[pl.ds((2 + p) * half, half), :] = w[p]


def sends_far_first():
    return (lax.axis_index("strm") // 2 == 0) == (lax.axis_index("band") % 2 == 1)


def far_comes_first():
    return (lax.axis_index("strm") // 2 == 0) == (lax.axis_index("band") % 2 == 0)


def at_end():
    place = lax.axis_index("band")
    return (place == 0) | (place == lax.axis_size("band") - 1)


def sum_kernel(half, own, one, other, two, *pieces):
    me, place, bands = lax.axis_index("strm"), lax.axis_index("band"), lax.axis_size("band")
    upper = me // 2 == 0
    outside = jnp.where(upper, place == bands - 1, place == 0)
    beyond = jnp.where(upper, place >= bands - 2, place <= 1)
    far_first = far_comes_first()
    alone = at_end()
    channels = pieces[0].shape[-1]
    for p in range(2):
        at = pl.ds(p * half, half)
        after = pl.ds((2 + p) * half, half)
        centre = own[at, :] + one[at, :].astype(f32) + jnp.where(alone, 0.0, other[at, :].astype(f32))
        extra = jnp.where(far_first, one[after, :].astype(f32), jnp.where(alone, 0.0, other[after, :].astype(f32)))
        extra = own[after, :] + extra + jnp.where(beyond, 0.0, two[at, :].astype(f32))
        extra = jnp.where(outside, 0.0, extra)
        for side in range(2):
            lanes = slice(side * channels, (side + 1) * channels)
            pieces[2 * p + side][pl.ds(0, half), :] = centre[:, lanes].astype(bf16)
            pieces[2 * p + side][pl.ds(half, half), :] = extra[:, lanes].astype(bf16)


def cache_kernel(columns, mid, one, other, w0, w1, w2, w3, sums, weights, first_taps):
    me = lax.axis_index("strm")
    upper = me // 2 == 0
    far_first = far_comes_first()
    channels = sums.shape[-1]
    group = channels // 4
    width = 2 * columns
    area = 2 * width
    for d, quarter in enumerate((w0, w1, w2, w3)):
        at = pl.ds(pl.multiple_of((me ^ d) * group, 16), group)
        values = quarter[...].reshape(14, group, 2 * channels)
        left, right = values[:, :, :channels], values[:13, :, channels:]
        first_taps[:, at, :] = left[:9]
        weights[pl.ds(0, 5), at, :] = left[9:]
        weights[pl.ds(5, 13), at, :] = right

    first_edge = one[pl.ds(4 * width, width), :].astype(f32)
    second_edge = jnp.where(at_end(), 0.0, other[pl.ds(4 * width, width), :].astype(f32))
    far = jnp.where(far_first, first_edge, second_edge)
    near = jnp.where(far_first, second_edge, first_edge)
    top = jnp.where(upper, near, far).astype(bf16)
    bottom = jnp.where(upper, far, near).astype(bf16)
    stored = jnp.concatenate([top, mid[...], bottom], axis=0)
    size = stored.shape[0]
    row = lax.broadcasted_iota(jnp.int32, (size, size), 0)
    column = lax.broadcasted_iota(jnp.int32, (size, size), 1)
    inside = row % width
    natural = 2 * (inside % columns) + inside // columns
    both = jnp.zeros((2 * area, channels), f32)
    early = jnp.zeros((area, channels), f32)
    for l in range(3):
        source = natural + (l - 1)
        keep = (source >= 0) & (source < width) & (column == row - inside + source)
        view = dot(jnp.where(keep, 1.0, 0.0).astype(bf16), stored).astype(bf16)
        c0, c1 = view[:, :channels], view[:, channels:]
        for j in range(3):
            at = slice(j * width, j * width + area)
            tap = 3 * j + l
            both = both + dot(jnp.concatenate([c0[at], c1[at]], axis=0), first_taps[tap], True)
            early = early + dot(c1[at], weights[tap], True)
    sums[0] = both[:area] + early
    sums[1] = both[area:]


def second_kernel(frames, columns, p0, p1, p2, p3, sums, weights, gain, out, quarters):
    me = lax.axis_index("strm")
    channels = out.shape[-1]
    width = 2 * columns
    for e, piece in enumerate((p0, p1, p2, p3)):
        quarters[me ^ e] = piece[...]

    fields = [quarters[q].astype(f32).reshape(2, frames, columns, channels) for q in range(4)]
    row_of = ((1, 1), (0, 0), (1, 0), (0, 1))
    upsampled = jnp.stack(
        [jnp.stack([jnp.stack([fields[2 * a + b][c, t] for b in range(2)]) for a, c in row_of]) for t in range(frames)]
    )
    act = norm_silu(upsampled.reshape(-1, channels), gain[...][None, :])
    left, same, right = [
        v.astype(bf16).reshape(frames, 4, 2, columns, channels) for v in shifted(act, columns)
    ]

    def split(first, second):
        return jnp.stack([first, second], axis=2)

    views = [
        split(left[:, :, 1], same[:, :, 0]),
        same,
        split(same[:, :, 1], right[:, :, 0]),
    ]
    area = 2 * width
    both = sums[...].reshape(2 * area, channels)
    late = jnp.zeros((area, channels), f32)
    for j in range(3):
        for l in range(3):
            window = views[l][:, j : j + 2].reshape(2 * area, channels)
            tap = 3 * j + l
            both = both + dot(window, weights[9 + tap], True)
            late = late + dot(window[:area], weights[tap], True)

    row = lax.broadcasted_iota(jnp.int32, (area, area), 0)
    column = lax.broadcasted_iota(jnp.int32, (area, area), 1)
    inside = row % width
    keep = column == row - inside + (inside % 2) * columns + inside // 2
    order = jnp.where(keep, 1.0, 0.0).astype(bf16)
    for t, branch in enumerate((both[:area], both[area:] + late)):
        base = upsampled[t, 1:3].reshape(area, channels)
        decoded = (base + branch.astype(bf16).astype(f32)).astype(bf16)
        out[0, t] = dot(order, decoded).astype(bf16).reshape(2, width, channels)


def whole(count):
    return [pl.BlockSpec(memory_space=pltpu.VMEM)] * count


THERE = pl.BlockSpec(memory_space=pltpu.HBM)


def there(value):
    return pltpu.with_memory_space_constraint(value, pltpu.HBM)


def call(kernel, name, megabytes, **settings):
    return pl.pallas_call(
        kernel, name=name, compiler_params=pltpu.CompilerParams(vmem_limit_bytes=megabytes * 2**20), **settings
    )


def struct(shape, dtype=bf16):
    return jax.ShapeDtypeStruct(shape, dtype)


def body(latents, cache_first, cache_second, gain_first, gain_second, w_first, w_second, cache_slot, block_index):
    frames, columns, channels = latents.shape[1], latents.shape[3], latents.shape[4]
    outputs = w_first.shape[-1]
    bands = lax.axis_size("band")
    streams = lax.axis_size("strm")
    assert streams == 4 and bands % 2 == 0 and latents.shape[2] == 1 and frames == 2
    half = frames * columns
    width = 2 * columns

    def swapped(value, distance):
        return lax.ppermute(value, "strm", [(i, i ^ distance) for i in range(streams)])

    def along(value, target):
        pairs = []
        for band in range(bands):
            for k in range(streams):
                to, there = target(band, k)
                if 0 <= to < bands:
                    pairs.append((band * streams + k, to * streams + there))
        return lax.ppermute(value, ("band", "strm"), pairs)

    def first_way(band, k):
        return band ^ 1, k

    def second_way(band, k):
        if band in (0, bands - 1):
            return band, k ^ 1
        return ((band + 1) ^ 1) - 1, k

    def third_way(band, k):
        if bands == 4:
            return band ^ 2, k
        return (band - 2 if k // 2 == 0 else band + 2), k

    turned_first = jnp.swapaxes(w_first, 3, 4)
    turned_second = jnp.swapaxes(w_second, 3, 4)
    group = turned_second.shape[3]
    packed = call(
        pack_kernel,
        "pack",
        4,
        out_shape=struct((2 * half + 2 * width, channels)),
        in_specs=[THERE] * 4,
        out_specs=whole(1)[0],
        scratch_shapes=[
            pltpu.VMEM(latents.shape, bf16),
            pltpu.VMEM(cache_first.shape, bf16),
            pltpu.VMEM(cache_second.shape, bf16),
            pltpu.VMEM(gain_first.shape, f32),
            pltpu.SemaphoreType.DMA((4,)),
        ],
    )(*map(there, (latents, cache_first, cache_second, gain_first)))
    across = swapped(packed, 2)
    weight_first, weight_own, masks = call(
        fetch_kernel,
        "fetch",
        16,
        out_shape=[struct(turned_first.shape), struct((14 * group, 2 * outputs)), struct((4, 4, 1, channels), f32)],
        in_specs=whole(1) + [THERE] * 4,
        out_specs=whole(3),
        scratch_shapes=[
            pltpu.VMEM(turned_second.shape, bf16),
            pltpu.SMEM(cache_slot.shape, jnp.int32),
            pltpu.SMEM(block_index.shape, jnp.int32),
            pltpu.SemaphoreType.DMA((4,)),
        ],
    )(packed, *map(there, (turned_first, turned_second, cache_slot, block_index)))
    weight_own, across = lax.optimization_barrier((weight_own, across))
    packs = [packed, swapped(packed, 1), across, swapped(across, 1)]
    weights = [weight_own, swapped(weight_own, 1), swapped(weight_own, 2)]
    pair = struct((2 * half, 2 * outputs))
    payload = struct((4 * half + width, 2 * outputs))
    one, other, two, own, mid = call(
        functools.partial(first_kernel, frames, columns),
        "first_conv",
        16,
        out_shape=[payload, payload, pair, struct((4 * half, 2 * outputs), f32), struct((2 * width, 2 * outputs))],
        in_specs=whole(6),
        out_specs=whole(5),
    )(*packs, weight_first, masks)
    one, other, two = along(one, first_way), along(other, second_way), along(two, third_way)
    pieces = call(
        functools.partial(sum_kernel, half),
        "row_sums",
        4,
        out_shape=[struct((2 * half, outputs))] * 4,
        in_specs=whole(4),
        out_specs=whole(4),
    )(own, one, other, two)
    weight_across, _ = lax.optimization_barrier((weights[2], pieces[0]))
    weights.append(swapped(weight_across, 1))
    pieces = [pieces[0]] + [swapped(pieces[d], d) for d in (1, 2, 3)]
    sums, taps = call(
        functools.partial(cache_kernel, columns),
        "cached_conv",
        16,
        out_shape=[struct((2, 2 * width, outputs), f32), struct((18, outputs, outputs))],
        in_specs=whole(7),
        out_specs=whole(2),
        scratch_shapes=[pltpu.VMEM((9, outputs, outputs), bf16)],
    )(mid, one, other, *weights)
    return call(
        functools.partial(second_kernel, frames, columns),
        "second_conv",
        16,
        out_shape=struct((1, frames, 2, width, outputs)),
        in_specs=whole(7),
        out_specs=whole(1)[0],
        scratch_shapes=[pltpu.VMEM((4, 2 * half, outputs), bf16)],
    )(*pieces, sums, taps, gain_second)


def solution(mesh):
    in_specs = (
        P(("grp", "strm"), None, "band", None, None),
        P(("grp", "strm"), None, "band", None, None),
        P(("grp", "strm"), None, "band", None, None),
        P(),
        P(),
        P(None, None, None, None, "strm"),
        P(None, None, None, None, "strm"),
        P("grp"),
        P("grp"),
    )
    out_specs = P(("grp", "strm"), None, "band", None, None)
    return jax.shard_map(body, mesh=mesh, in_specs=in_specs, out_specs=out_specs, check_vma=False)
```

```python
import functools

import jax
import jax.numpy as jnp
from jax import lax
from jax.experimental import pallas as pl
from jax.experimental.pallas import tpu as pltpu
from jax.sharding import PartitionSpec as P

epsilon = 1e-06
f32 = jnp.float32
bf16 = jnp.bfloat16


def norm_silu(values, gain):
    mean_square = jnp.mean(values * values, axis=-1, keepdims=True)
    return jax.nn.silu(values * lax.rsqrt(mean_square + epsilon) * gain)


def dot(lhs, rhs, transposed=False):
    dims = (((1,), (1,)), ((), ())) if transposed else (((1,), (0,)), ((), ()))
    return lax.dot_general(lhs, rhs, dims, preferred_element_type=f32)


def shifted(values, width):
    count = values.shape[0]
    place = lax.broadcasted_iota(jnp.int32, values.shape, 0) % width
    left = jnp.where(place == 0, 0.0, pltpu.roll(values, 1, 0))
    right = jnp.where(place == width - 1, 0.0, pltpu.roll(values, count - 1, 0))
    return left, values, right


def halves(values):
    count = values.shape[0] // 2
    return jnp.concatenate([values[:count], values[count:]], axis=1)


def pack_kernel(latents, first, second, gain_there, out, latent_here, first_here, second_here, gain, sems):
    loads = [
        pltpu.make_async_copy(*pair, sems.at[n])
        for n, pair in enumerate(((gain_there, gain), (latents, latent_here), (first, first_here), (second, second_here)))
    ]
    for load in loads:
        load.start()
    rows, channels = latent_here.shape[1] * latent_here.shape[3], latent_here.shape[-1]
    width = second_here.shape[3]
    for load in loads:
        load.wait()
    out[pl.ds(0, rows), :] = first_here[...].reshape(rows, channels)
    act = norm_silu(latent_here[...].reshape(rows, channels).astype(f32), gain[...][None, :])
    out[pl.ds(rows, rows), :] = act.astype(bf16)
    for r in range(2):
        out[pl.ds(2 * rows + r * width, width), :] = jnp.concatenate([second_here[0, f, r] for f in range(2)], axis=1)


def fetch_kernel(
    packed, first_there, second_there, slots_there, blocks_there, first, second, masks, second_here, slots, blocks, sems
):
    del packed
    loads = [
        pltpu.make_async_copy(second_there, second_here, sems.at[0]),
        pltpu.make_async_copy(slots_there, slots, sems.at[1]),
        pltpu.make_async_copy(blocks_there, blocks, sems.at[2]),
        pltpu.make_async_copy(first_there, first, sems.at[3]),
    ]
    for load in loads:
        load.start()
    for load in loads[:3]:
        load.wait()
    me = lax.axis_index("strm")
    for d in range(4):
        for e in range(4):
            chosen = (slots[me ^ d] == me ^ e) & (blocks[me ^ d] > 0)
            masks[d, e] = jnp.full(masks.shape[2:], jnp.where(chosen, 1.0, 0.0), f32)
    taps, group, channels = 27, second_here.shape[-2], second_here.shape[-1]
    values = second_here[...].reshape(taps * group, channels)
    most = (taps + 1) // 2 * group
    rest = taps * group - most
    second[pl.ds(0, rest), :] = jnp.concatenate([values[:rest], values[most:]], axis=1)
    last = values[rest:most]
    second[pl.ds(rest, group), :] = jnp.concatenate([last, last], axis=1)
    loads[3].wait()


def first_kernel(frames, columns, p0, p1, p2, p3, weight, masks, one, other, two, own, mid):
    packs = (p0, p1, p2, p3)
    upper = lax.axis_index("strm") // 2 == 0
    channels = p0.shape[-1]
    outputs = weight.shape[-2]
    half = frames * columns
    width = 2 * columns

    def chosen(d, at):
        return sum(jnp.where(masks[d, e] > 0.5, packs[e][at, :].astype(f32), 0.0) for e in range(4))

    parts = []
    for d in range(4):
        parts.append(chosen(d, pl.ds(0, half)))
        parts.append(packs[d][pl.ds(half, half), :].astype(f32))
    views = [
        view.astype(bf16).reshape(4, frames + 2, columns, channels)
        for view in shifted(jnp.concatenate(parts, axis=0), columns)
    ]
    rows = 4 * half
    sums = [jnp.zeros((rows, outputs), f32) for _ in range(3)]
    taps = [jnp.where(upper, 2, 0), 1, jnp.where(upper, 0, 2)]
    for i in range(3):
        for l in range(3):
            window = views[l][:, i : i + frames].reshape(rows, channels)
            for j in range(3):
                sums[j] = sums[j] + dot(window, weight[i, taps[j], l], True)

    u, v, w = [[halves(values[: 2 * half]), halves(values[2 * half :])] for values in sums]
    far_first = sends_far_first()
    cached = chosen(0, pl.ds(2 * half, 2 * width))
    mid[...] = cached.astype(bf16)
    edges = [cached[:width], cached[width:]]
    far = u + v + [jnp.where(upper, edges[0], edges[1])]
    near = w + [jnp.zeros_like(w[0])] * 2 + [jnp.where(upper, edges[1], edges[0])]
    for n in range(5):
        at = pl.ds(n * half, half)
        one[at, :] = jnp.where(far_first, far[n], near[n]).astype(bf16)
        other[at, :] = jnp.where(far_first, near[n], far[n]).astype(bf16)
    for p in range(2):
        two[pl.ds(p * half, half), :] = u[p].astype(bf16)
        own[pl.ds(p * half, half), :] = v[p]
        own[pl.ds((2 + p) * half, half), :] = w[p]


def sends_far_first():
    return (lax.axis_index("strm") // 2 == 0) == (lax.axis_index("band") % 2 == 1)


def far_comes_first():
    return (lax.axis_index("strm") // 2 == 0) == (lax.axis_index("band") % 2 == 0)


def at_end():
    place = lax.axis_index("band")
    return (place == 0) | (place == lax.axis_size("band") - 1)


def sum_kernel(half, own, one, other, two, *pieces):
    me, place, bands = lax.axis_index("strm"), lax.axis_index("band"), lax.axis_size("band")
    upper = me // 2 == 0
    outside = jnp.where(upper, place == bands - 1, place == 0)
    beyond = jnp.where(upper, place >= bands - 2, place <= 1)
    far_first = far_comes_first()
    alone = at_end()
    channels = pieces[0].shape[-1]
    for p in range(2):
        at = pl.ds(p * half, half)
        after = pl.ds((2 + p) * half, half)
        centre = own[at, :] + one[at, :].astype(f32) + jnp.where(alone, 0.0, other[at, :].astype(f32))
        extra = jnp.where(far_first, one[after, :].astype(f32), jnp.where(alone, 0.0, other[after, :].astype(f32)))
        extra = own[after, :] + extra + jnp.where(beyond, 0.0, two[at, :].astype(f32))
        extra = jnp.where(outside, 0.0, extra)
        for side in range(2):
            lanes = slice(side * channels, (side + 1) * channels)
            pieces[2 * p + side][pl.ds(0, half), :] = centre[:, lanes].astype(bf16)
            pieces[2 * p + side][pl.ds(half, half), :] = extra[:, lanes].astype(bf16)


def cache_kernel(columns, mid, one, other, w0, w1, w2, w3, sums, weights, first_taps):
    me = lax.axis_index("strm")
    upper = me // 2 == 0
    far_first = far_comes_first()
    channels = sums.shape[-1]
    group = channels // 4
    width = 2 * columns
    area = 2 * width
    for d, quarter in enumerate((w0, w1, w2, w3)):
        at = pl.ds(pl.multiple_of((me ^ d) * group, 16), group)
        values = quarter[...].reshape(14, group, 2 * channels)
        left, right = values[:, :, :channels], values[:13, :, channels:]
        first_taps[:, at, :] = left[:9]
        weights[pl.ds(0, 5), at, :] = left[9:]
        weights[pl.ds(5, 13), at, :] = right

    first_edge = one[pl.ds(4 * width, width), :].astype(f32)
    second_edge = jnp.where(at_end(), 0.0, other[pl.ds(4 * width, width), :].astype(f32))
    far = jnp.where(far_first, first_edge, second_edge)
    near = jnp.where(far_first, second_edge, first_edge)
    top = jnp.where(upper, near, far).astype(bf16)
    bottom = jnp.where(upper, far, near).astype(bf16)
    stored = jnp.concatenate([top, mid[...], bottom], axis=0)
    size = stored.shape[0]
    row = lax.broadcasted_iota(jnp.int32, (size, size), 0)
    column = lax.broadcasted_iota(jnp.int32, (size, size), 1)
    inside = row % width
    natural = 2 * (inside % columns) + inside // columns
    both = jnp.zeros((2 * area, channels), f32)
    early = jnp.zeros((area, channels), f32)
    for l in range(3):
        source = natural + (l - 1)
        keep = (source >= 0) & (source < width) & (column == row - inside + source)
        view = dot(jnp.where(keep, 1.0, 0.0).astype(bf16), stored).astype(bf16)
        c0, c1 = view[:, :channels], view[:, channels:]
        for j in range(3):
            at = slice(j * width, j * width + area)
            tap = 3 * j + l
            both = both + dot(jnp.concatenate([c0[at], c1[at]], axis=0), first_taps[tap], True)
            early = early + dot(c1[at], weights[tap], True)
    sums[0] = both[:area] + early
    sums[1] = both[area:]


def second_kernel(frames, columns, p0, p1, p2, p3, sums, weights, gain, out, quarters):
    me = lax.axis_index("strm")
    channels = out.shape[-1]
    width = 2 * columns
    for e, piece in enumerate((p0, p1, p2, p3)):
        quarters[me ^ e] = piece[...]

    fields = [quarters[q].astype(f32).reshape(2, frames, columns, channels) for q in range(4)]
    row_of = ((1, 1), (0, 0), (1, 0), (0, 1))
    upsampled = jnp.stack(
        [jnp.stack([jnp.stack([fields[2 * a + b][c, t] for b in range(2)]) for a, c in row_of]) for t in range(frames)]
    )
    act = norm_silu(upsampled.reshape(-1, channels), gain[...][None, :])
    left, same, right = [
        v.astype(bf16).reshape(frames, 4, 2, columns, channels) for v in shifted(act, columns)
    ]

    def split(first, second):
        return jnp.stack([first, second], axis=2)

    views = [
        split(left[:, :, 1], same[:, :, 0]),
        same,
        split(same[:, :, 1], right[:, :, 0]),
    ]
    area = 2 * width
    both = sums[...].reshape(2 * area, channels)
    late = jnp.zeros((area, channels), f32)
    for j in range(3):
        for l in range(3):
            window = views[l][:, j : j + 2].reshape(2 * area, channels)
            tap = 3 * j + l
            both = both + dot(window, weights[9 + tap], True)
            late = late + dot(window[:area], weights[tap], True)

    row = lax.broadcasted_iota(jnp.int32, (area, area), 0)
    column = lax.broadcasted_iota(jnp.int32, (area, area), 1)
    inside = row % width
    keep = column == row - inside + (inside % 2) * columns + inside // 2
    order = jnp.where(keep, 1.0, 0.0).astype(bf16)
    for t, branch in enumerate((both[:area], both[area:] + late)):
        base = upsampled[t, 1:3].reshape(area, channels)
        decoded = (base + branch.astype(bf16).astype(f32)).astype(bf16)
        out[0, t] = dot(order, decoded).astype(bf16).reshape(2, width, channels)


def whole(count):
    return [pl.BlockSpec(memory_space=pltpu.VMEM)] * count


THERE = pl.BlockSpec(memory_space=pltpu.HBM)


def there(value):
    return pltpu.with_memory_space_constraint(value, pltpu.HBM)


def call(kernel, name, megabytes, microseconds=1, **settings):
    cost = pl.CostEstimate(flops=int(microseconds * 1e9), bytes_accessed=0, transcendentals=0)
    return pl.pallas_call(
        kernel, name=name, cost_estimate=cost, compiler_params=pltpu.CompilerParams(vmem_limit_bytes=megabytes * 2**20), **settings
    )


def struct(shape, dtype=bf16):
    return jax.ShapeDtypeStruct(shape, dtype)


def body(latents, cache_first, cache_second, gain_first, gain_second, w_first, w_second, cache_slot, block_index):
    frames, columns, channels = latents.shape[1], latents.shape[3], latents.shape[4]
    outputs = w_first.shape[-1]
    bands = lax.axis_size("band")
    streams = lax.axis_size("strm")
    assert streams == 4 and bands % 2 == 0 and latents.shape[2] == 1 and frames == 2
    half = frames * columns
    width = 2 * columns

    def swapped(value, distance):
        return lax.ppermute(value, "strm", [(i, i ^ distance) for i in range(streams)])

    def along(value, target):
        pairs = []
        for band in range(bands):
            for k in range(streams):
                to, there = target(band, k)
                if 0 <= to < bands:
                    pairs.append((band * streams + k, to * streams + there))
        return lax.ppermute(value, ("band", "strm"), pairs)

    def first_way(band, k):
        return band ^ 1, k

    def second_way(band, k):
        if band in (0, bands - 1):
            return band, k ^ 1
        return ((band + 1) ^ 1) - 1, k

    def third_way(band, k):
        if bands == 4:
            return band ^ 2, k
        return (band - 2 if k // 2 == 0 else band + 2), k

    turned_first = jnp.swapaxes(w_first, 3, 4)
    turned_second = jnp.swapaxes(w_second, 3, 4)
    group = turned_second.shape[3]
    packed = call(
        pack_kernel,
        "pack",
        4,
        out_shape=struct((2 * half + 2 * width, channels)),
        in_specs=[THERE] * 4,
        out_specs=whole(1)[0],
        scratch_shapes=[
            pltpu.VMEM(latents.shape, bf16),
            pltpu.VMEM(cache_first.shape, bf16),
            pltpu.VMEM(cache_second.shape, bf16),
            pltpu.VMEM(gain_first.shape, f32),
            pltpu.SemaphoreType.DMA((4,)),
        ],
    )(*map(there, (latents, cache_first, cache_second, gain_first)))
    across = swapped(packed, 2)
    weight_first, weight_own, masks = call(
        fetch_kernel,
        "fetch",
        16,
        0.05,
        out_shape=[struct(turned_first.shape), struct((14 * group, 2 * outputs)), struct((4, 4, 1, channels), f32)],
        in_specs=whole(1) + [THERE] * 4,
        out_specs=whole(3),
        scratch_shapes=[
            pltpu.VMEM(turned_second.shape, bf16),
            pltpu.SMEM(cache_slot.shape, jnp.int32),
            pltpu.SMEM(block_index.shape, jnp.int32),
            pltpu.SemaphoreType.DMA((4,)),
        ],
    )(packed, *map(there, (turned_first, turned_second, cache_slot, block_index)))
    weight_first, across = lax.optimization_barrier((weight_first, across))
    packs = [packed, swapped(packed, 1), across, swapped(across, 1)]
    weights = [weight_own, swapped(weight_own, 1), swapped(weight_own, 2)]
    pair = struct((2 * half, 2 * outputs))
    payload = struct((4 * half + width, 2 * outputs))
    one, other, two, own, mid = call(
        functools.partial(first_kernel, frames, columns),
        "first_conv",
        16,
        2,
        out_shape=[payload, payload, pair, struct((4 * half, 2 * outputs), f32), struct((2 * width, 2 * outputs))],
        in_specs=whole(6),
        out_specs=whole(5),
    )(*packs, weight_first, masks)
    one, other, two = along(one, first_way), along(other, second_way), along(two, third_way)
    pieces = call(
        functools.partial(sum_kernel, half),
        "row_sums",
        4,
        1,
        out_shape=[struct((2 * half, outputs))] * 4,
        in_specs=whole(4),
        out_specs=whole(4),
    )(own, one, other, two)
    weight_across, _ = lax.optimization_barrier((weights[2], pieces[0]))
    weights.append(swapped(weight_across, 1))
    across, beyond = swapped(pieces[2], 2), swapped(pieces[3], 3)
    sums, taps = call(
        functools.partial(cache_kernel, columns),
        "cached_conv",
        16,
        1,
        out_shape=[struct((2, 2 * width, outputs), f32), struct((18, outputs, outputs))],
        in_specs=whole(7),
        out_specs=whole(2),
        scratch_shapes=[pltpu.VMEM((9, outputs, outputs), bf16)],
    )(mid, one, other, *weights)
    beside, sums = lax.optimization_barrier((pieces[1], sums))
    pieces = [pieces[0], swapped(beside, 1), across, beyond]
    return call(
        functools.partial(second_kernel, frames, columns),
        "second_conv",
        16,
        out_shape=struct((1, frames, 2, width, outputs)),
        in_specs=whole(7),
        out_specs=whole(1)[0],
        scratch_shapes=[pltpu.VMEM((4, 2 * half, outputs), bf16)],
    )(*pieces, sums, taps, gain_second)


def solution(mesh):
    in_specs = (
        P(("grp", "strm"), None, "band", None, None),
        P(("grp", "strm"), None, "band", None, None),
        P(("grp", "strm"), None, "band", None, None),
        P(),
        P(),
        P(None, None, None, None, "strm"),
        P(None, None, None, None, "strm"),
        P("grp"),
        P("grp"),
    )
    out_specs = P(("grp", "strm"), None, "band", None, None)
    return jax.shard_map(body, mesh=mesh, in_specs=in_specs, out_specs=out_specs, check_vma=False)
```

```python
import functools

import jax
import jax.numpy as jnp
from jax import lax
from jax.experimental import pallas as pl
from jax.experimental.pallas import tpu as pltpu
from jax.sharding import PartitionSpec as P

epsilon = 1e-06
f32 = jnp.float32
bf16 = jnp.bfloat16


def norm_silu(values, gain):
    mean_square = jnp.mean(values * values, axis=-1, keepdims=True)
    return jax.nn.silu(values * lax.rsqrt(mean_square + epsilon) * gain)


def dot(lhs, rhs, transposed=False):
    dims = (((1,), (1,)), ((), ())) if transposed else (((1,), (0,)), ((), ()))
    return lax.dot_general(lhs, rhs, dims, preferred_element_type=f32)


def shifted(values, width):
    count = values.shape[0]
    place = lax.broadcasted_iota(jnp.int32, values.shape, 0) % width
    left = jnp.where(place == 0, 0.0, pltpu.roll(values, 1, 0))
    right = jnp.where(place == width - 1, 0.0, pltpu.roll(values, count - 1, 0))
    return left, values, right


def halves(values):
    count = values.shape[0] // 2
    return jnp.concatenate([values[:count], values[count:]], axis=1)


def pack_kernel(latents, first, second, gain_there, out, latent_here, first_here, second_here, gain, sems):
    loads = [
        pltpu.make_async_copy(*pair, sems.at[n])
        for n, pair in enumerate(((gain_there, gain), (latents, latent_here), (first, first_here), (second, second_here)))
    ]
    for load in loads:
        load.start()
    rows, channels = latent_here.shape[1] * latent_here.shape[3], latent_here.shape[-1]
    width = second_here.shape[3]
    for load in loads:
        load.wait()
    out[pl.ds(0, rows), :] = first_here[...].reshape(rows, channels)
    act = norm_silu(latent_here[...].reshape(rows, channels).astype(f32), gain[...][None, :])
    out[pl.ds(rows, rows), :] = act.astype(bf16)
    for r in range(2):
        out[pl.ds(2 * rows + r * width, width), :] = jnp.concatenate([second_here[0, f, r] for f in range(2)], axis=1)


def fetch_kernel(
    packed, first_there, second_there, slots_there, blocks_there, first, second, masks, second_here, slots, blocks, sems
):
    del packed
    loads = [
        pltpu.make_async_copy(second_there, second_here, sems.at[0]),
        pltpu.make_async_copy(slots_there, slots, sems.at[1]),
        pltpu.make_async_copy(blocks_there, blocks, sems.at[2]),
        pltpu.make_async_copy(first_there, first, sems.at[3]),
    ]
    for load in loads:
        load.start()
    for load in loads[:3]:
        load.wait()
    me = lax.axis_index("strm")
    for d in range(4):
        for e in range(4):
            chosen = (slots[me ^ d] == me ^ e) & (blocks[me ^ d] > 0)
            masks[d, e] = jnp.full(masks.shape[2:], jnp.where(chosen, 1.0, 0.0), f32)
    taps, group, channels = 27, second_here.shape[-2], second_here.shape[-1]
    values = second_here[...].reshape(taps * group, channels)
    most = (taps + 1) // 2 * group
    second[pl.ds(0, taps * group), :] = values[:, :128]
    right = jnp.concatenate([values[most:, 128:], values[:group, 128:]], axis=0)
    second[pl.ds(taps * group, most), :] = jnp.concatenate([values[:most, 128:], right], axis=1)
    loads[3].wait()


def first_kernel(frames, columns, p0, p1, p2, p3, weight, masks, one, other, two, own, mid):
    packs = (p0, p1, p2, p3)
    upper = lax.axis_index("strm") // 2 == 0
    channels = p0.shape[-1]
    outputs = weight.shape[-2]
    half = frames * columns
    width = 2 * columns

    def chosen(d, at):
        return sum(jnp.where(masks[d, e] > 0.5, packs[e][at, :].astype(f32), 0.0) for e in range(4))

    parts = []
    for d in range(4):
        parts.append(chosen(d, pl.ds(0, half)))
        parts.append(packs[d][pl.ds(half, half), :].astype(f32))
    views = [
        view.astype(bf16).reshape(4, frames + 2, columns, channels)
        for view in shifted(jnp.concatenate(parts, axis=0), columns)
    ]
    rows = 4 * half
    sums = [jnp.zeros((rows, outputs), f32) for _ in range(3)]
    taps = [jnp.where(upper, 2, 0), 1, jnp.where(upper, 0, 2)]
    for i in range(3):
        window = jnp.concatenate([view[:, i : i + frames].reshape(rows, channels) for view in views], axis=1)
        for j in range(3):
            kernel = jnp.concatenate([weight[i, taps[j], l] for l in range(3)], axis=1)
            sums[j] = sums[j] + dot(window, kernel, True)

    u, v, w = [[halves(values[: 2 * half]), halves(values[2 * half :])] for values in sums]
    far_first = sends_far_first()
    cached = chosen(0, pl.ds(2 * half, 2 * width))
    mid[...] = cached.astype(bf16)
    edges = [cached[:width], cached[width:]]
    far = u + v + [jnp.where(upper, edges[0], edges[1])]
    near = w + [jnp.zeros_like(w[0])] * 2 + [jnp.where(upper, edges[1], edges[0])]
    for n in range(5):
        at = pl.ds(n * half, half)
        one[at, :] = jnp.where(far_first, far[n], near[n]).astype(bf16)
        other[at, :] = jnp.where(far_first, near[n], far[n]).astype(bf16)
    for p in range(2):
        two[pl.ds(p * half, half), :] = u[p].astype(bf16)
        own[pl.ds(p * half, half), :] = v[p]
        own[pl.ds((2 + p) * half, half), :] = w[p]


def sends_far_first():
    return (lax.axis_index("strm") // 2 == 0) == (lax.axis_index("band") % 2 == 0)


def far_comes_first():
    return (lax.axis_index("strm") // 2 == 0) == (lax.axis_index("band") % 2 == 1)


def at_end():
    place = lax.axis_index("band")
    return (place == 0) | (place == lax.axis_size("band") - 1)


def sum_kernel(half, own, one, other, two, *pieces):
    me, place, bands = lax.axis_index("strm"), lax.axis_index("band"), lax.axis_size("band")
    upper = me // 2 == 0
    outside = jnp.where(upper, place == bands - 1, place == 0)
    beyond = jnp.where(upper, place >= bands - 2, place <= 1)
    far_first = far_comes_first()
    alone = at_end()
    channels = pieces[0].shape[-1]
    for p in range(2):
        at = pl.ds(p * half, half)
        after = pl.ds((2 + p) * half, half)
        centre = own[at, :] + other[at, :].astype(f32) + jnp.where(alone, 0.0, one[at, :].astype(f32))
        extra = jnp.where(far_first, jnp.where(alone, 0.0, one[after, :].astype(f32)), other[after, :].astype(f32))
        extra = own[after, :] + extra + jnp.where(beyond, 0.0, two[at, :].astype(f32))
        extra = jnp.where(outside, 0.0, extra)
        for side in range(2):
            lanes = slice(side * channels, (side + 1) * channels)
            pieces[2 * p + side][pl.ds(0, half), :] = centre[:, lanes].astype(bf16)
            pieces[2 * p + side][pl.ds(half, half), :] = extra[:, lanes].astype(bf16)


def view_kernel(columns, mid, one, other, views):
    upper = lax.axis_index("strm") // 2 == 0
    far_first = far_comes_first()
    width = 2 * columns
    first_edge = jnp.where(at_end(), 0.0, one[pl.ds(4 * width, width), :].astype(f32))
    second_edge = other[pl.ds(4 * width, width), :].astype(f32)
    far = jnp.where(far_first, first_edge, second_edge)
    near = jnp.where(far_first, second_edge, first_edge)
    top = jnp.where(upper, near, far).astype(bf16)
    bottom = jnp.where(upper, far, near).astype(bf16)
    stored = jnp.concatenate([top, mid[...], bottom], axis=0)
    size = stored.shape[0]
    row = lax.broadcasted_iota(jnp.int32, (size, size), 0)
    column = lax.broadcasted_iota(jnp.int32, (size, size), 1)
    inside = row % width
    natural = 2 * (inside % columns) + inside // columns
    for l in range(3):
        source = natural + (l - 1)
        keep = (source >= 0) & (source < width) & (column == row - inside + source)
        views[l] = dot(jnp.where(keep, 1.0, 0.0).astype(bf16), stored).astype(bf16)


def cache_kernel(columns, views, w0, w1, w2, w3, sums, weights, first_taps):
    me = lax.axis_index("strm")
    channels = sums.shape[-1]
    group = channels // 4
    width = 2 * columns
    area = 2 * width
    for d, quarter in enumerate((w0, w1, w2, w3)):
        at = pl.ds(pl.multiple_of((me ^ d) * group, 16), group)
        first_taps[:, at, pl.ds(0, 128)] = quarter[pl.ds(0, 9 * group), :].reshape(9, group, 128)
        weights[:, at, pl.ds(0, 128)] = quarter[pl.ds(9 * group, 18 * group), :].reshape(18, group, 128)
        others = quarter[pl.ds(27 * group, 14 * group), :].reshape(14, group, 128)
        first_taps[:, at, pl.ds(128, 64)] = others[:9, :, :64]
        weights[pl.ds(0, 5), at, pl.ds(128, 64)] = others[9:, :, :64]
        weights[pl.ds(5, 13), at, pl.ds(128, 64)] = others[:13, :, 64:]

    both = jnp.zeros((2 * area, channels), f32)
    early = jnp.zeros((area, channels), f32)
    for l in range(3):
        c0, c1 = views[l, :, :channels], views[l, :, channels:]
        for j in range(3):
            at = slice(j * width, j * width + area)
            tap = 3 * j + l
            both = both + dot(jnp.concatenate([c0[at], c1[at]], axis=0), first_taps[tap], True)
            early = early + dot(c1[at], weights[tap], True)
    sums[0] = both[:area] + early
    sums[1] = both[area:]


def second_kernel(frames, columns, p0, p1, p2, p3, sums, weights, gain, out, quarters):
    me = lax.axis_index("strm")
    channels = out.shape[-1]
    width = 2 * columns
    for e, piece in enumerate((p0, p1, p2, p3)):
        quarters[me ^ e] = piece[...]

    fields = [quarters[q].astype(f32).reshape(2, frames, columns, channels) for q in range(4)]
    row_of = ((1, 1), (0, 0), (1, 0), (0, 1))
    upsampled = jnp.stack(
        [jnp.stack([jnp.stack([fields[2 * a + b][c, t] for b in range(2)]) for a, c in row_of]) for t in range(frames)]
    )
    act = norm_silu(upsampled.reshape(-1, channels), gain[...][None, :])
    left, same, right = [
        v.astype(bf16).reshape(frames, 4, 2, columns, channels) for v in shifted(act, columns)
    ]

    def split(first, second):
        return jnp.stack([first, second], axis=2)

    views = [
        split(left[:, :, 1], same[:, :, 0]),
        same,
        split(same[:, :, 1], right[:, :, 0]),
    ]
    area = 2 * width
    both = sums[...].reshape(2 * area, channels)
    late = jnp.zeros((area, channels), f32)
    for j in range(3):
        for l in range(3):
            window = views[l][:, j : j + 2].reshape(2 * area, channels)
            tap = 3 * j + l
            both = both + dot(window, weights[9 + tap], True)
            late = late + dot(window[:area], weights[tap], True)

    row = lax.broadcasted_iota(jnp.int32, (area, area), 0)
    column = lax.broadcasted_iota(jnp.int32, (area, area), 1)
    inside = row % width
    keep = column == row - inside + (inside % 2) * columns + inside // 2
    order = jnp.where(keep, 1.0, 0.0).astype(bf16)
    for t, branch in enumerate((both[:area], both[area:] + late)):
        base = upsampled[t, 1:3].reshape(area, channels)
        decoded = (base + branch.astype(bf16).astype(f32)).astype(bf16)
        out[0, t] = dot(order, decoded).astype(bf16).reshape(2, width, channels)


def whole(count):
    return [pl.BlockSpec(memory_space=pltpu.VMEM)] * count


THERE = pl.BlockSpec(memory_space=pltpu.HBM)


def there(value):
    return pltpu.with_memory_space_constraint(value, pltpu.HBM)


def call(kernel, name, megabytes, microseconds=1, **settings):
    cost = pl.CostEstimate(flops=int(microseconds * 1e9), bytes_accessed=0, transcendentals=0)
    return pl.pallas_call(
        kernel, name=name, cost_estimate=cost, compiler_params=pltpu.CompilerParams(vmem_limit_bytes=megabytes * 2**20), **settings
    )


def struct(shape, dtype=bf16):
    return jax.ShapeDtypeStruct(shape, dtype)


def body(latents, cache_first, cache_second, gain_first, gain_second, w_first, w_second, cache_slot, block_index):
    frames, columns, channels = latents.shape[1], latents.shape[3], latents.shape[4]
    outputs = w_first.shape[-1]
    bands = lax.axis_size("band")
    streams = lax.axis_size("strm")
    assert outputs == 192 and streams == 4 and bands % 2 == 0 and latents.shape[2] == 1 and frames == 2
    half = frames * columns
    width = 2 * columns

    def swapped(value, distance):
        return lax.ppermute(value, "strm", [(i, i ^ distance) for i in range(streams)])

    def along(value, target):
        pairs = []
        for band in range(bands):
            for k in range(streams):
                to, there = target(band, k)
                if 0 <= to < bands:
                    pairs.append((band * streams + k, to * streams + there))
        return lax.ppermute(value, ("band", "strm"), pairs)

    def first_way(band, k):
        return band ^ 1, k

    def second_way(band, k):
        if band in (0, bands - 1):
            return band, k ^ 1
        return ((band + 1) ^ 1) - 1, k

    def third_way(band, k):
        if bands == 4:
            return band ^ 2, k
        return (band - 2 if k // 2 == 0 else band + 2), k

    turned_first = jnp.swapaxes(w_first, 3, 4)
    turned_second = jnp.swapaxes(w_second, 3, 4)
    group = turned_second.shape[3]
    packed = call(
        pack_kernel,
        "pack",
        4,
        out_shape=struct((2 * half + 2 * width, channels)),
        in_specs=[THERE] * 4,
        out_specs=whole(1)[0],
        scratch_shapes=[
            pltpu.VMEM(latents.shape, bf16),
            pltpu.VMEM(cache_first.shape, bf16),
            pltpu.VMEM(cache_second.shape, bf16),
            pltpu.VMEM(gain_first.shape, f32),
            pltpu.SemaphoreType.DMA((4,)),
        ],
    )(*map(there, (latents, cache_first, cache_second, gain_first)))
    across = swapped(packed, 2)
    weight_first, weight_own, masks = call(
        fetch_kernel,
        "fetch",
        16,
        0.05,
        out_shape=[struct(turned_first.shape), struct((41 * group, 128)), struct((4, 4, 1, channels), f32)],
        in_specs=whole(1) + [THERE] * 4,
        out_specs=whole(3),
        scratch_shapes=[
            pltpu.VMEM(turned_second.shape, bf16),
            pltpu.SMEM(cache_slot.shape, jnp.int32),
            pltpu.SMEM(block_index.shape, jnp.int32),
            pltpu.SemaphoreType.DMA((4,)),
        ],
    )(packed, *map(there, (turned_first, turned_second, cache_slot, block_index)))
    weight_first, across = lax.optimization_barrier((weight_first, across))
    packs = [packed, swapped(packed, 1), across, swapped(across, 1)]
    weights = [weight_own, swapped(weight_own, 1), swapped(weight_own, 2)]
    pair = struct((2 * half, 2 * outputs))
    payload = struct((4 * half + width, 2 * outputs))
    one, other, two, own, mid = call(
        functools.partial(first_kernel, frames, columns),
        "first_conv",
        16,
        1.5,
        out_shape=[payload, payload, pair, struct((4 * half, 2 * outputs), f32), struct((2 * width, 2 * outputs))],
        in_specs=whole(6),
        out_specs=whole(5),
    )(*packs, weight_first, masks)
    one, other, two = along(one, second_way), along(other, first_way), along(two, third_way)
    pieces = call(
        functools.partial(sum_kernel, half),
        "row_sums",
        4,
        1,
        out_shape=[struct((2 * half, outputs))] * 4,
        in_specs=whole(4),
        out_specs=whole(4),
    )(own, one, other, two)
    across, beyond = swapped(pieces[2], 2), swapped(pieces[3], 3)
    mid, one, other, _ = lax.optimization_barrier((mid, one, other, pieces[0]))
    views = call(
        functools.partial(view_kernel, columns),
        "cached_views",
        4,
        0.1,
        out_shape=struct((3, 4 * width, 2 * outputs)),
        in_specs=whole(3),
        out_specs=whole(1)[0],
    )(mid, one, other)
    weight_across, views = lax.optimization_barrier((weights[2], views))
    weights.append(swapped(weight_across, 1))
    sums, taps = call(
        functools.partial(cache_kernel, columns),
        "cached_conv",
        16,
        1,
        out_shape=[struct((2, 2 * width, outputs), f32), struct((18, outputs, outputs))],
        in_specs=whole(5),
        out_specs=whole(2),
        scratch_shapes=[pltpu.VMEM((9, outputs, outputs), bf16)],
    )(views, *weights)
    beside, sums = lax.optimization_barrier((pieces[1], sums))
    pieces = [pieces[0], swapped(beside, 1), across, beyond]
    return call(
        functools.partial(second_kernel, frames, columns),
        "second_conv",
        16,
        out_shape=struct((1, frames, 2, width, outputs)),
        in_specs=whole(7),
        out_specs=whole(1)[0],
        scratch_shapes=[pltpu.VMEM((4, 2 * half, outputs), bf16)],
    )(*pieces, sums, taps, gain_second)


def solution(mesh):
    in_specs = (
        P(("grp", "strm"), None, "band", None, None),
        P(("grp", "strm"), None, "band", None, None),
        P(("grp", "strm"), None, "band", None, None),
        P(),
        P(),
        P(None, None, None, None, "strm"),
        P(None, None, None, None, "strm"),
        P("grp"),
        P("grp"),
    )
    out_specs = P(("grp", "strm"), None, "band", None, None)
    return jax.shard_map(body, mesh=mesh, in_specs=in_specs, out_specs=out_specs, check_vma=False)
```

```python
import functools

import jax
import jax.numpy as jnp
from jax import lax
from jax.experimental import pallas as pl
from jax.experimental.pallas import tpu as pltpu
from jax.sharding import PartitionSpec as P

epsilon = 1e-06
f32 = jnp.float32
bf16 = jnp.bfloat16


def norm_silu(values, gain):
    mean_square = jnp.mean(values * values, axis=-1, keepdims=True)
    return jax.nn.silu(values * lax.rsqrt(mean_square + epsilon) * gain)


def dot(lhs, rhs, transposed=False):
    dims = (((1,), (1,)), ((), ())) if transposed else (((1,), (0,)), ((), ()))
    return lax.dot_general(lhs, rhs, dims, preferred_element_type=f32)


def shifted(values, width):
    count = values.shape[0]
    place = lax.broadcasted_iota(jnp.int32, values.shape, 0) % width
    left = jnp.where(place == 0, 0.0, pltpu.roll(values, 1, 0))
    right = jnp.where(place == width - 1, 0.0, pltpu.roll(values, count - 1, 0))
    return left, values, right


def halves(values):
    count = values.shape[0] // 2
    return jnp.concatenate([values[:count], values[count:]], axis=1)


def pack_kernel(latents, first, second, gain_there, out, latent_here, first_here, second_here, gain, sems):
    loads = [
        pltpu.make_async_copy(*pair, sems.at[n])
        for n, pair in enumerate(((gain_there, gain), (latents, latent_here), (first, first_here), (second, second_here)))
    ]
    for load in loads:
        load.start()
    rows, channels = latent_here.shape[1] * latent_here.shape[3], latent_here.shape[-1]
    width = second_here.shape[3]
    for load in loads:
        load.wait()
    out[pl.ds(0, rows), :] = first_here[...].reshape(rows, channels)
    act = norm_silu(latent_here[...].reshape(rows, channels).astype(f32), gain[...][None, :])
    out[pl.ds(rows, rows), :] = act.astype(bf16)
    for r in range(2):
        out[pl.ds(2 * rows + r * width, width), :] = jnp.concatenate([second_here[0, f, r] for f in range(2)], axis=1)


def fetch_kernel(
    packed, first_there, second_here, slots_there, blocks_there, first, second, masks, slots, blocks, sems
):
    del packed
    loads = [
        pltpu.make_async_copy(slots_there, slots, sems.at[0]),
        pltpu.make_async_copy(blocks_there, blocks, sems.at[1]),
        pltpu.make_async_copy(first_there, first, sems.at[2]),
    ]
    for load in loads:
        load.start()
    for load in loads[:2]:
        load.wait()
    me = lax.axis_index("strm")
    for d in range(4):
        for e in range(4):
            chosen = (slots[me ^ d] == me ^ e) & (blocks[me ^ d] > 0)
            masks[d, e] = jnp.full(masks.shape[2:], jnp.where(chosen, 1.0, 0.0), f32)
    taps, group, channels = 27, second_here.shape[-2], second_here.shape[-1]
    values = second_here[...].reshape(taps * group, channels)
    most = (taps + 1) // 2 * group
    second[pl.ds(0, taps * group), :] = values[:, :128]
    right = jnp.concatenate([values[most:, 128:], values[:group, 128:]], axis=0)
    second[pl.ds(taps * group, most), :] = jnp.concatenate([values[:most, 128:], right], axis=1)
    loads[2].wait()


def first_kernel(frames, columns, p0, p1, p2, p3, weight, masks, one, other, two, own, mid):
    packs = (p0, p1, p2, p3)
    upper = lax.axis_index("strm") // 2 == 0
    channels = p0.shape[-1]
    outputs = weight.shape[-2]
    half = frames * columns
    width = 2 * columns

    def chosen(d, at):
        return sum(jnp.where(masks[d, e] > 0.5, packs[e][at, :].astype(f32), 0.0) for e in range(4))

    parts = []
    for d in range(4):
        parts.append(chosen(d, pl.ds(0, half)))
        parts.append(packs[d][pl.ds(half, half), :].astype(f32))
    views = [
        view.astype(bf16).reshape(4, frames + 2, columns, channels)
        for view in shifted(jnp.concatenate(parts, axis=0), columns)
    ]
    rows = 4 * half
    sums = [jnp.zeros((rows, outputs), f32) for _ in range(3)]
    taps = [jnp.where(upper, 2, 0), 1, jnp.where(upper, 0, 2)]
    for i in range(3):
        window = jnp.concatenate([view[:, i : i + frames].reshape(rows, channels) for view in views], axis=1)
        for j in range(3):
            kernel = jnp.concatenate([weight[i, taps[j], l] for l in range(3)], axis=1)
            sums[j] = sums[j] + dot(window, kernel, True)

    u, v, w = [[halves(values[: 2 * half]), halves(values[2 * half :])] for values in sums]
    far_first = sends_far_first()
    cached = chosen(0, pl.ds(2 * half, 2 * width))
    mid[...] = cached.astype(bf16)
    edges = [cached[:width], cached[width:]]
    far = u + v + [jnp.where(upper, edges[0], edges[1])]
    near = w + [jnp.zeros_like(w[0])] * 2 + [jnp.where(upper, edges[1], edges[0])]
    for n in range(5):
        at = pl.ds(n * half, half)
        one[at, :] = jnp.where(far_first, far[n], near[n]).astype(bf16)
        other[at, :] = jnp.where(far_first, near[n], far[n]).astype(bf16)
    for p in range(2):
        two[pl.ds(p * half, half), :] = u[p].astype(bf16)
        own[pl.ds(p * half, half), :] = v[p]
        own[pl.ds((2 + p) * half, half), :] = w[p]


def sends_far_first():
    return (lax.axis_index("strm") // 2 == 0) == (lax.axis_index("band") % 2 == 0)


def far_comes_first():
    return (lax.axis_index("strm") // 2 == 0) == (lax.axis_index("band") % 2 == 1)


def at_end():
    place = lax.axis_index("band")
    return (place == 0) | (place == lax.axis_size("band") - 1)


def sum_kernel(half, own, one, other, two, *pieces):
    me, place, bands = lax.axis_index("strm"), lax.axis_index("band"), lax.axis_size("band")
    upper = me // 2 == 0
    outside = jnp.where(upper, place == bands - 1, place == 0)
    beyond = jnp.where(upper, place >= bands - 2, place <= 1)
    far_first = far_comes_first()
    alone = at_end()
    channels = pieces[0].shape[-1] // 2
    for p in range(2):
        at = pl.ds(p * half, half)
        after = pl.ds((2 + p) * half, half)
        centre = own[at, :] + other[at, :].astype(f32) + jnp.where(alone, 0.0, one[at, :].astype(f32))
        extra = jnp.where(far_first, jnp.where(alone, 0.0, one[after, :].astype(f32)), other[after, :].astype(f32))
        extra = own[after, :] + extra + jnp.where(beyond, 0.0, two[at, :].astype(f32))
        extra = jnp.where(outside, 0.0, extra)
        for side in range(2):
            lanes = slice(side * channels, (side + 1) * channels)
            both = jnp.concatenate([centre[:, lanes], extra[:, lanes]], axis=1)
            pieces[2 * p + side][...] = both.astype(bf16)


def view_kernel(columns, mid, one, other, views):
    upper = lax.axis_index("strm") // 2 == 0
    far_first = far_comes_first()
    width = 2 * columns
    first_edge = jnp.where(at_end(), 0.0, one[pl.ds(4 * width, width), :].astype(f32))
    second_edge = other[pl.ds(4 * width, width), :].astype(f32)
    far = jnp.where(far_first, first_edge, second_edge)
    near = jnp.where(far_first, second_edge, first_edge)
    top = jnp.where(upper, near, far).astype(bf16)
    bottom = jnp.where(upper, far, near).astype(bf16)
    stored = jnp.concatenate([top, mid[...], bottom], axis=0)
    size = stored.shape[0]
    row = lax.broadcasted_iota(jnp.int32, (size, size), 0)
    column = lax.broadcasted_iota(jnp.int32, (size, size), 1)
    inside = row % width
    natural = 2 * (inside % columns) + inside // columns
    for l in range(3):
        source = natural + (l - 1)
        keep = (source >= 0) & (source < width) & (column == row - inside + source)
        views[l] = dot(jnp.where(keep, 1.0, 0.0).astype(bf16), stored).astype(bf16)


def cache_kernel(columns, views, w0, w1, w2, w3, sums, weights, first_taps):
    me = lax.axis_index("strm")
    channels = sums.shape[-1]
    group = channels // 4
    width = 2 * columns
    area = 2 * width
    for d, quarter in enumerate((w0, w1, w2, w3)):
        at = pl.ds(pl.multiple_of((me ^ d) * group, 16), group)
        first_taps[:, at, pl.ds(0, 128)] = quarter[pl.ds(0, 9 * group), :].reshape(9, group, 128)
        weights[:, at, pl.ds(0, 128)] = quarter[pl.ds(9 * group, 18 * group), :].reshape(18, group, 128)
        others = quarter[pl.ds(27 * group, 14 * group), :].reshape(14, group, 128)
        first_taps[:, at, pl.ds(128, 64)] = others[:9, :, :64]
        weights[pl.ds(0, 5), at, pl.ds(128, 64)] = others[9:, :, :64]
        weights[pl.ds(5, 13), at, pl.ds(128, 64)] = others[:13, :, 64:]

    both = jnp.zeros((2 * area, channels), f32)
    early = jnp.zeros((area, channels), f32)
    for l in range(3):
        c0, c1 = views[l, :, :channels], views[l, :, channels:]
        for j in range(3):
            at = slice(j * width, j * width + area)
            tap = 3 * j + l
            both = both + dot(jnp.concatenate([c0[at], c1[at]], axis=0), first_taps[tap], True)
            early = early + dot(c1[at], weights[tap], True)
    sums[0] = both[:area] + early
    sums[1] = both[area:]


def second_kernel(frames, columns, p0, p1, p2, p3, sums, weights, gain, out, quarters):
    me = lax.axis_index("strm")
    channels = out.shape[-1]
    width = 2 * columns
    for e, piece in enumerate((p0, p1, p2, p3)):
        quarters[me ^ e, 0] = piece[:, :channels]
        quarters[me ^ e, 1] = piece[:, channels:]

    fields = [quarters[q].astype(f32).reshape(2, frames, columns, channels) for q in range(4)]
    row_of = ((1, 1), (0, 0), (1, 0), (0, 1))
    upsampled = jnp.stack(
        [jnp.stack([jnp.stack([fields[2 * a + b][c, t] for b in range(2)]) for a, c in row_of]) for t in range(frames)]
    )
    act = norm_silu(upsampled.reshape(-1, channels), gain[...][None, :])
    left, same, right = [
        v.astype(bf16).reshape(frames, 4, 2, columns, channels) for v in shifted(act, columns)
    ]

    def split(first, second):
        return jnp.stack([first, second], axis=2)

    views = [
        split(left[:, :, 1], same[:, :, 0]),
        same,
        split(same[:, :, 1], right[:, :, 0]),
    ]
    area = 2 * width
    both = sums[...].reshape(2 * area, channels)
    late = jnp.zeros((area, channels), f32)
    for j in range(3):
        for l in range(3):
            window = views[l][:, j : j + 2].reshape(2 * area, channels)
            tap = 3 * j + l
            both = both + dot(window, weights[9 + tap], True)
            late = late + dot(window[:area], weights[tap], True)

    row = lax.broadcasted_iota(jnp.int32, (area, area), 0)
    column = lax.broadcasted_iota(jnp.int32, (area, area), 1)
    inside = row % width
    keep = column == row - inside + (inside % 2) * columns + inside // 2
    order = jnp.where(keep, 1.0, 0.0).astype(bf16)
    for t, branch in enumerate((both[:area], both[area:] + late)):
        base = upsampled[t, 1:3].reshape(area, channels)
        decoded = (base + branch.astype(bf16).astype(f32)).astype(bf16)
        out[0, t] = dot(order, decoded).astype(bf16).reshape(2, width, channels)


def whole(count):
    return [pl.BlockSpec(memory_space=pltpu.VMEM)] * count


THERE = pl.BlockSpec(memory_space=pltpu.HBM)


def there(value):
    return pltpu.with_memory_space_constraint(value, pltpu.HBM)


def call(kernel, name, megabytes, microseconds=1, **settings):
    cost = pl.CostEstimate(flops=int(microseconds * 1e9), bytes_accessed=0, transcendentals=0)
    return pl.pallas_call(
        kernel, name=name, cost_estimate=cost, compiler_params=pltpu.CompilerParams(vmem_limit_bytes=megabytes * 2**20), **settings
    )


def struct(shape, dtype=bf16):
    return jax.ShapeDtypeStruct(shape, dtype)


def body(latents, cache_first, cache_second, gain_first, gain_second, w_first, w_second, cache_slot, block_index):
    frames, columns, channels = latents.shape[1], latents.shape[3], latents.shape[4]
    outputs = w_first.shape[-1]
    bands = lax.axis_size("band")
    streams = lax.axis_size("strm")
    assert outputs == 192 and streams == 4 and bands % 2 == 0 and latents.shape[2] == 1 and frames == 2
    half = frames * columns
    width = 2 * columns

    def swapped(value, distance):
        return lax.ppermute(value, "strm", [(i, i ^ distance) for i in range(streams)])

    def along(value, target):
        pairs = []
        for band in range(bands):
            for k in range(streams):
                to, there = target(band, k)
                if 0 <= to < bands:
                    pairs.append((band * streams + k, to * streams + there))
        return lax.ppermute(value, ("band", "strm"), pairs)

    def first_way(band, k):
        return band ^ 1, k

    def second_way(band, k):
        if band in (0, bands - 1):
            return band, k ^ 1
        return ((band + 1) ^ 1) - 1, k

    def third_way(band, k):
        if bands == 4:
            return band ^ 2, k
        return (band - 2 if k // 2 == 0 else band + 2), k

    turned_first = jnp.swapaxes(w_first, 3, 4)
    turned_second = jnp.swapaxes(w_second, 3, 4)
    group = turned_second.shape[3]
    packed = call(
        pack_kernel,
        "pack",
        4,
        5,
        out_shape=struct((2 * half + 2 * width, channels)),
        in_specs=[THERE] * 4,
        out_specs=whole(1)[0],
        scratch_shapes=[
            pltpu.VMEM(latents.shape, bf16),
            pltpu.VMEM(cache_first.shape, bf16),
            pltpu.VMEM(cache_second.shape, bf16),
            pltpu.VMEM(gain_first.shape, f32),
            pltpu.SemaphoreType.DMA((4,)),
        ],
    )(*map(there, (latents, cache_first, cache_second, gain_first)))
    across = swapped(packed, 2)
    weight_first, weight_own, masks = call(
        fetch_kernel,
        "fetch",
        16,
        0.05,
        out_shape=[struct(turned_first.shape), struct((41 * group, 128)), struct((4, 4, 1, channels), f32)],
        in_specs=whole(1) + [THERE] + whole(1) + [THERE] * 2,
        out_specs=whole(3),
        scratch_shapes=[
            pltpu.SMEM(cache_slot.shape, jnp.int32),
            pltpu.SMEM(block_index.shape, jnp.int32),
            pltpu.SemaphoreType.DMA((3,)),
        ],
    )(packed, there(turned_first), turned_second, there(cache_slot), there(block_index))
    weight_first, across = lax.optimization_barrier((weight_first, across))
    packs = [packed, swapped(packed, 1), across, swapped(across, 1)]
    weights = [weight_own, swapped(weight_own, 1), swapped(weight_own, 2)]
    pair = struct((2 * half, 2 * outputs))
    payload = struct((4 * half + width, 2 * outputs))
    one, other, two, own, mid = call(
        functools.partial(first_kernel, frames, columns),
        "first_conv",
        16,
        1.5,
        out_shape=[payload, payload, pair, struct((4 * half, 2 * outputs), f32), struct((2 * width, 2 * outputs))],
        in_specs=whole(6),
        out_specs=whole(5),
    )(*packs, weight_first, masks)
    one, other, two = along(one, second_way), along(other, first_way), along(two, third_way)
    pieces = call(
        functools.partial(sum_kernel, half),
        "row_sums",
        4,
        1,
        out_shape=[struct((half, 2 * outputs))] * 4,
        in_specs=whole(4),
        out_specs=whole(4),
    )(own, one, other, two)
    across, beyond = swapped(pieces[2], 2), swapped(pieces[3], 3)
    mid, one, other, _ = lax.optimization_barrier((mid, one, other, pieces[0]))
    views = call(
        functools.partial(view_kernel, columns),
        "cached_views",
        4,
        0.1,
        out_shape=struct((3, 4 * width, 2 * outputs)),
        in_specs=whole(3),
        out_specs=whole(1)[0],
    )(mid, one, other)
    weight_across, views = lax.optimization_barrier((weights[2], views))
    weights.append(swapped(weight_across, 1))
    sums, taps = call(
        functools.partial(cache_kernel, columns),
        "cached_conv",
        16,
        1,
        out_shape=[struct((2, 2 * width, outputs), f32), struct((18, outputs, outputs))],
        in_specs=whole(5),
        out_specs=whole(2),
        scratch_shapes=[pltpu.VMEM((9, outputs, outputs), bf16)],
    )(views, *weights)
    beside, sums = lax.optimization_barrier((pieces[1], sums))
    pieces = [pieces[0], swapped(beside, 1), across, beyond]
    return call(
        functools.partial(second_kernel, frames, columns),
        "second_conv",
        16,
        out_shape=struct((1, frames, 2, width, outputs)),
        in_specs=whole(7),
        out_specs=whole(1)[0],
        scratch_shapes=[pltpu.VMEM((4, 2, half, outputs), bf16)],
    )(*pieces, sums, taps, gain_second)


def solution(mesh):
    in_specs = (
        P(("grp", "strm"), None, "band", None, None),
        P(("grp", "strm"), None, "band", None, None),
        P(("grp", "strm"), None, "band", None, None),
        P(),
        P(),
        P(None, None, None, None, "strm"),
        P(None, None, None, None, "strm"),
        P("grp"),
        P("grp"),
    )
    out_specs = P(("grp", "strm"), None, "band", None, None)
    return jax.shard_map(body, mesh=mesh, in_specs=in_specs, out_specs=out_specs, check_vma=False)
```

```python
import functools

import jax
import jax.numpy as jnp
from jax import lax
from jax.experimental import pallas as pl
from jax.experimental.pallas import tpu as pltpu
from jax.sharding import PartitionSpec as P

epsilon = 1e-06
f32 = jnp.float32
bf16 = jnp.bfloat16


def norm_silu(values, gain):
    mean_square = jnp.mean(values * values, axis=-1, keepdims=True)
    return jax.nn.silu(values * lax.rsqrt(mean_square + epsilon) * gain)


def dot(lhs, rhs, transposed=False):
    dims = (((1,), (1,)), ((), ())) if transposed else (((1,), (0,)), ((), ()))
    return lax.dot_general(lhs, rhs, dims, preferred_element_type=f32)


def shifted(values, width):
    count = values.shape[0]
    place = lax.broadcasted_iota(jnp.int32, values.shape, 0) % width
    left = jnp.where(place == 0, 0.0, pltpu.roll(values, 1, 0))
    right = jnp.where(place == width - 1, 0.0, pltpu.roll(values, count - 1, 0))
    return left, values, right


def halves(values):
    count = values.shape[0] // 2
    return jnp.concatenate([values[:count], values[count:]], axis=1)


def pack_kernel(latents, first, second, gain_there, out, latent_here, first_here, second_here, gain, sems):
    loads = [
        pltpu.make_async_copy(*pair, sems.at[n])
        for n, pair in enumerate(((gain_there, gain), (latents, latent_here), (first, first_here), (second, second_here)))
    ]
    for load in loads:
        load.start()
    rows, channels = latent_here.shape[1] * latent_here.shape[3], latent_here.shape[-1]
    width = second_here.shape[3]
    for load in loads:
        load.wait()
    out[pl.ds(0, rows), :] = first_here[...].reshape(rows, channels)
    act = norm_silu(latent_here[...].reshape(rows, channels).astype(f32), gain[...][None, :])
    out[pl.ds(rows, rows), :] = act.astype(bf16)
    for r in range(2):
        out[pl.ds(2 * rows + r * width, width), :] = jnp.concatenate([second_here[0, f, r] for f in range(2)], axis=1)


def fetch_kernel(
    packed, first_there, second_here, slots_there, blocks_there, first, second, masks, slots, blocks, sems
):
    del packed
    loads = [
        pltpu.make_async_copy(slots_there, slots, sems.at[0]),
        pltpu.make_async_copy(blocks_there, blocks, sems.at[1]),
        pltpu.make_async_copy(first_there, first, sems.at[2]),
    ]
    for load in loads:
        load.start()
    for load in loads[:2]:
        load.wait()
    me = lax.axis_index("strm")
    for d in range(4):
        for e in range(4):
            chosen = (slots[me ^ d] == me ^ e) & (blocks[me ^ d] > 0)
            masks[d, e] = jnp.full(masks.shape[2:], jnp.where(chosen, 1.0, 0.0), f32)
    taps, group, channels = 27, second_here.shape[-2], second_here.shape[-1]
    values = second_here[...].reshape(taps * group, channels)
    most = (taps + 1) // 2 * group
    second[pl.ds(0, taps * group), :] = values[:, :128]
    right = jnp.concatenate([values[most:, 128:], values[:group, 128:]], axis=0)
    second[pl.ds(taps * group, most), :] = jnp.concatenate([values[:most, 128:], right], axis=1)
    loads[2].wait()


def first_kernel(frames, columns, p0, p1, p2, p3, weight, masks, one, other, two, own, mid):
    packs = (p0, p1, p2, p3)
    upper = lax.axis_index("strm") // 2 == 0
    channels = p0.shape[-1]
    outputs = weight.shape[-2]
    half = frames * columns
    width = 2 * columns

    def chosen(d, at):
        return sum(jnp.where(masks[d, e] > 0.5, packs[e][at, :].astype(f32), 0.0) for e in range(4))

    parts = []
    for d in range(4):
        parts.append(chosen(d, pl.ds(0, half)))
        parts.append(packs[d][pl.ds(half, half), :].astype(f32))
    views = [
        view.astype(bf16).reshape(4, frames + 2, columns, channels)
        for view in shifted(jnp.concatenate(parts, axis=0), columns)
    ]
    rows = 4 * half
    turned = jnp.zeros((3 * outputs, rows), f32)
    taps = [jnp.where(upper, 2, 0), 1, jnp.where(upper, 0, 2)]
    for i in range(3):
        window = jnp.concatenate([view[:, i : i + frames].reshape(rows, channels) for view in views], axis=1)
        kernel = jnp.concatenate(
            [jnp.concatenate([weight[i, taps[j], l] for l in range(3)], axis=1) for j in range(3)], axis=0
        )
        turned = turned + dot(kernel, window, True)

    sums = [turned[j * outputs : (j + 1) * outputs].T for j in range(3)]
    u, v, w = [[halves(values[: 2 * half]), halves(values[2 * half :])] for values in sums]
    far_first = sends_far_first()
    cached = chosen(0, pl.ds(2 * half, 2 * width))
    mid[...] = cached.astype(bf16)
    edges = [cached[:width], cached[width:]]
    far = u + v + [jnp.where(upper, edges[0], edges[1])]
    near = w + [jnp.zeros_like(w[0])] * 2 + [jnp.where(upper, edges[1], edges[0])]
    for n in range(5):
        at = pl.ds(n * half, half)
        one[at, :] = jnp.where(far_first, far[n], near[n]).astype(bf16)
        other[at, :] = jnp.where(far_first, near[n], far[n]).astype(bf16)
    for p in range(2):
        two[pl.ds(p * half, half), :] = u[p].astype(bf16)
        own[pl.ds(p * half, half), :] = v[p]
        own[pl.ds((2 + p) * half, half), :] = w[p]


def sends_far_first():
    return (lax.axis_index("strm") // 2 == 0) == (lax.axis_index("band") % 2 == 0)


def far_comes_first():
    return (lax.axis_index("strm") // 2 == 0) == (lax.axis_index("band") % 2 == 1)


def at_end():
    place = lax.axis_index("band")
    return (place == 0) | (place == lax.axis_size("band") - 1)


def sum_kernel(half, own, one, other, two, *pieces):
    me, place, bands = lax.axis_index("strm"), lax.axis_index("band"), lax.axis_size("band")
    upper = me // 2 == 0
    outside = jnp.where(upper, place == bands - 1, place == 0)
    beyond = jnp.where(upper, place >= bands - 2, place <= 1)
    far_first = far_comes_first()
    alone = at_end()
    channels = pieces[0].shape[-1] // 2
    for p in range(2):
        at = pl.ds(p * half, half)
        after = pl.ds((2 + p) * half, half)
        centre = own[at, :] + other[at, :].astype(f32) + jnp.where(alone, 0.0, one[at, :].astype(f32))
        extra = jnp.where(far_first, jnp.where(alone, 0.0, one[after, :].astype(f32)), other[after, :].astype(f32))
        extra = own[after, :] + extra + jnp.where(beyond, 0.0, two[at, :].astype(f32))
        extra = jnp.where(outside, 0.0, extra)
        for side in range(2):
            lanes = slice(side * channels, (side + 1) * channels)
            both = jnp.concatenate([centre[:, lanes], extra[:, lanes]], axis=1)
            pieces[2 * p + side][...] = both.astype(bf16)


def view_kernel(columns, mid, one, other, views):
    upper = lax.axis_index("strm") // 2 == 0
    far_first = far_comes_first()
    width = 2 * columns
    first_edge = jnp.where(at_end(), 0.0, one[pl.ds(4 * width, width), :].astype(f32))
    second_edge = other[pl.ds(4 * width, width), :].astype(f32)
    far = jnp.where(far_first, first_edge, second_edge)
    near = jnp.where(far_first, second_edge, first_edge)
    top = jnp.where(upper, near, far).astype(bf16)
    bottom = jnp.where(upper, far, near).astype(bf16)
    stored = jnp.concatenate([top, mid[...], bottom], axis=0)
    size = stored.shape[0]
    row = lax.broadcasted_iota(jnp.int32, (size, size), 0)
    column = lax.broadcasted_iota(jnp.int32, (size, size), 1)
    inside = row % width
    natural = 2 * (inside % columns) + inside // columns
    for l in range(3):
        source = natural + (l - 1)
        keep = (source >= 0) & (source < width) & (column == row - inside + source)
        views[l] = dot(jnp.where(keep, 1.0, 0.0).astype(bf16), stored).astype(bf16)


def cache_kernel(columns, views, w0, w1, w2, w3, sums, weights, first_taps):
    me = lax.axis_index("strm")
    channels = sums.shape[-1]
    group = channels // 4
    width = 2 * columns
    area = 2 * width
    for d, quarter in enumerate((w0, w1, w2, w3)):
        at = pl.ds(pl.multiple_of((me ^ d) * group, 16), group)
        first_taps[:, at, pl.ds(0, 128)] = quarter[pl.ds(0, 9 * group), :].reshape(9, group, 128)
        weights[:, at, pl.ds(0, 128)] = quarter[pl.ds(9 * group, 18 * group), :].reshape(18, group, 128)
        others = quarter[pl.ds(27 * group, 14 * group), :].reshape(14, group, 128)
        first_taps[:, at, pl.ds(128, 64)] = others[:9, :, :64]
        weights[pl.ds(0, 5), at, pl.ds(128, 64)] = others[9:, :, :64]
        weights[pl.ds(5, 13), at, pl.ds(128, 64)] = others[:13, :, 64:]

    both = jnp.zeros((2 * area, channels), f32)
    early = jnp.zeros((area, channels), f32)
    for l in range(3):
        c0, c1 = views[l, :, :channels], views[l, :, channels:]
        for j in range(3):
            at = slice(j * width, j * width + area)
            tap = 3 * j + l
            both = both + dot(jnp.concatenate([c0[at], c1[at]], axis=0), first_taps[tap], True)
            early = early + dot(c1[at], weights[tap], True)
    sums[0] = both[:area] + early
    sums[1] = both[area:]


def second_kernel(frames, columns, p0, p1, p2, p3, sums, weights, gain, out, quarters):
    me = lax.axis_index("strm")
    channels = out.shape[-1]
    width = 2 * columns
    for e, piece in enumerate((p0, p1, p2, p3)):
        quarters[me ^ e, 0] = piece[:, :channels]
        quarters[me ^ e, 1] = piece[:, channels:]

    fields = [quarters[q].astype(f32).reshape(2, frames, columns, channels) for q in range(4)]
    row_of = ((1, 1), (0, 0), (1, 0), (0, 1))
    upsampled = jnp.stack(
        [jnp.stack([jnp.stack([fields[2 * a + b][c, t] for b in range(2)]) for a, c in row_of]) for t in range(frames)]
    )
    act = norm_silu(upsampled.reshape(-1, channels), gain[...][None, :])
    left, same, right = [
        v.astype(bf16).reshape(frames, 4, 2, columns, channels) for v in shifted(act, columns)
    ]

    def split(first, second):
        return jnp.stack([first, second], axis=2)

    views = [
        split(left[:, :, 1], same[:, :, 0]),
        same,
        split(same[:, :, 1], right[:, :, 0]),
    ]
    area = 2 * width
    both = sums[...].reshape(2 * area, channels)
    late = jnp.zeros((area, channels), f32)
    for j in range(3):
        for l in range(3):
            window = views[l][:, j : j + 2].reshape(2 * area, channels)
            tap = 3 * j + l
            both = both + dot(window, weights[9 + tap], True)
            late = late + dot(window[:area], weights[tap], True)

    row = lax.broadcasted_iota(jnp.int32, (area, area), 0)
    column = lax.broadcasted_iota(jnp.int32, (area, area), 1)
    inside = row % width
    keep = column == row - inside + (inside % 2) * columns + inside // 2
    order = jnp.where(keep, 1.0, 0.0).astype(bf16)
    for t, branch in enumerate((both[:area], both[area:] + late)):
        base = upsampled[t, 1:3].reshape(area, channels)
        decoded = (base + branch.astype(bf16).astype(f32)).astype(bf16)
        out[0, t] = dot(order, decoded).astype(bf16).reshape(2, width, channels)


def whole(count):
    return [pl.BlockSpec(memory_space=pltpu.VMEM)] * count


THERE = pl.BlockSpec(memory_space=pltpu.HBM)


def there(value):
    return pltpu.with_memory_space_constraint(value, pltpu.HBM)


def call(kernel, name, megabytes, microseconds=1, **settings):
    cost = pl.CostEstimate(flops=int(microseconds * 1e9), bytes_accessed=0, transcendentals=0)
    return pl.pallas_call(
        kernel, name=name, cost_estimate=cost, compiler_params=pltpu.CompilerParams(vmem_limit_bytes=megabytes * 2**20), **settings
    )


def struct(shape, dtype=bf16):
    return jax.ShapeDtypeStruct(shape, dtype)


def body(latents, cache_first, cache_second, gain_first, gain_second, w_first, w_second, cache_slot, block_index):
    frames, columns, channels = latents.shape[1], latents.shape[3], latents.shape[4]
    outputs = w_first.shape[-1]
    bands = lax.axis_size("band")
    streams = lax.axis_size("strm")
    assert outputs == 192 and streams == 4 and bands % 2 == 0 and latents.shape[2] == 1 and frames == 2
    half = frames * columns
    width = 2 * columns

    def swapped(value, distance):
        return lax.ppermute(value, "strm", [(i, i ^ distance) for i in range(streams)])

    def along(value, target):
        pairs = []
        for band in range(bands):
            for k in range(streams):
                to, there = target(band, k)
                if 0 <= to < bands:
                    pairs.append((band * streams + k, to * streams + there))
        return lax.ppermute(value, ("band", "strm"), pairs)

    def first_way(band, k):
        return band ^ 1, k

    def second_way(band, k):
        if band in (0, bands - 1):
            return band, k ^ 1
        return ((band + 1) ^ 1) - 1, k

    def third_way(band, k):
        if bands == 4:
            return band ^ 2, k
        return (band - 2 if k // 2 == 0 else band + 2), k

    turned_first = jnp.swapaxes(w_first, 3, 4)
    turned_second = jnp.swapaxes(w_second, 3, 4)
    group = turned_second.shape[3]
    packed = call(
        pack_kernel,
        "pack",
        4,
        5,
        out_shape=struct((2 * half + 2 * width, channels)),
        in_specs=[THERE] * 4,
        out_specs=whole(1)[0],
        scratch_shapes=[
            pltpu.VMEM(latents.shape, bf16),
            pltpu.VMEM(cache_first.shape, bf16),
            pltpu.VMEM(cache_second.shape, bf16),
            pltpu.VMEM(gain_first.shape, f32),
            pltpu.SemaphoreType.DMA((4,)),
        ],
    )(*map(there, (latents, cache_first, cache_second, gain_first)))
    across = swapped(packed, 2)
    weight_first, weight_own, masks = call(
        fetch_kernel,
        "fetch",
        16,
        0.05,
        out_shape=[struct(turned_first.shape), struct((41 * group, 128)), struct((4, 4, 1, channels), f32)],
        in_specs=whole(1) + [THERE] + whole(1) + [THERE] * 2,
        out_specs=whole(3),
        scratch_shapes=[
            pltpu.SMEM(cache_slot.shape, jnp.int32),
            pltpu.SMEM(block_index.shape, jnp.int32),
            pltpu.SemaphoreType.DMA((3,)),
        ],
    )(packed, there(turned_first), turned_second, there(cache_slot), there(block_index))
    weight_first, across = lax.optimization_barrier((weight_first, across))
    packs = [packed, swapped(packed, 1), across, swapped(across, 1)]
    weights = [weight_own, swapped(weight_own, 1), swapped(weight_own, 2)]
    pair = struct((2 * half, 2 * outputs))
    payload = struct((4 * half + width, 2 * outputs))
    one, other, two, own, mid = call(
        functools.partial(first_kernel, frames, columns),
        "first_conv",
        16,
        1.5,
        out_shape=[payload, payload, pair, struct((4 * half, 2 * outputs), f32), struct((2 * width, 2 * outputs))],
        in_specs=whole(6),
        out_specs=whole(5),
    )(*packs, weight_first, masks)
    one, other, two = along(one, second_way), along(other, first_way), along(two, third_way)
    pieces = call(
        functools.partial(sum_kernel, half),
        "row_sums",
        4,
        1,
        out_shape=[struct((half, 2 * outputs))] * 4,
        in_specs=whole(4),
        out_specs=whole(4),
    )(own, one, other, two)
    across, beyond = swapped(pieces[2], 2), swapped(pieces[3], 3)
    mid, one, other, _ = lax.optimization_barrier((mid, one, other, pieces[0]))
    views = call(
        functools.partial(view_kernel, columns),
        "cached_views",
        4,
        0.1,
        out_shape=struct((3, 4 * width, 2 * outputs)),
        in_specs=whole(3),
        out_specs=whole(1)[0],
    )(mid, one, other)
    weight_across, views = lax.optimization_barrier((weights[2], views))
    weights.append(swapped(weight_across, 1))
    sums, taps = call(
        functools.partial(cache_kernel, columns),
        "cached_conv",
        16,
        1,
        out_shape=[struct((2, 2 * width, outputs), f32), struct((18, outputs, outputs))],
        in_specs=whole(5),
        out_specs=whole(2),
        scratch_shapes=[pltpu.VMEM((9, outputs, outputs), bf16)],
    )(views, *weights)
    beside, sums = lax.optimization_barrier((pieces[1], sums))
    pieces = [pieces[0], swapped(beside, 1), across, beyond]
    return call(
        functools.partial(second_kernel, frames, columns),
        "second_conv",
        16,
        out_shape=struct((1, frames, 2, width, outputs)),
        in_specs=whole(7),
        out_specs=whole(1)[0],
        scratch_shapes=[pltpu.VMEM((4, 2, half, outputs), bf16)],
    )(*pieces, sums, taps, gain_second)


def solution(mesh):
    in_specs = (
        P(("grp", "strm"), None, "band", None, None),
        P(("grp", "strm"), None, "band", None, None),
        P(("grp", "strm"), None, "band", None, None),
        P(),
        P(),
        P(None, None, None, None, "strm"),
        P(None, None, None, None, "strm"),
        P("grp"),
        P("grp"),
    )
    out_specs = P(("grp", "strm"), None, "band", None, None)
    return jax.shard_map(body, mesh=mesh, in_specs=in_specs, out_specs=out_specs, check_vma=False)
```

```python
import functools

import jax
import jax.numpy as jnp
from jax import lax
from jax.experimental import pallas as pl
from jax.experimental.pallas import tpu as pltpu
from jax.sharding import PartitionSpec as P

epsilon = 1e-06
f32 = jnp.float32
bf16 = jnp.bfloat16


def norm_silu(values, gain):
    mean_square = jnp.mean(values * values, axis=-1, keepdims=True)
    return jax.nn.silu(values * lax.rsqrt(mean_square + epsilon) * gain)


def dot(lhs, rhs, transposed=False):
    dims = (((1,), (1,)), ((), ())) if transposed else (((1,), (0,)), ((), ()))
    return lax.dot_general(lhs, rhs, dims, preferred_element_type=f32)


def shifted(values, width):
    count = values.shape[0]
    place = lax.broadcasted_iota(jnp.int32, values.shape, 0) % width
    left = jnp.where(place == 0, 0.0, pltpu.roll(values, 1, 0))
    right = jnp.where(place == width - 1, 0.0, pltpu.roll(values, count - 1, 0))
    return left, values, right


def halves(values):
    count = values.shape[0] // 2
    return jnp.concatenate([values[:count], values[count:]], axis=1)


def pack_kernel(latents, first, second, gain_there, out, latent_here, first_here, second_here, gain, sems):
    loads = [
        pltpu.make_async_copy(*pair, sems.at[n])
        for n, pair in enumerate(((gain_there, gain), (latents, latent_here), (first, first_here), (second, second_here)))
    ]
    for load in loads:
        load.start()
    rows, channels = latent_here.shape[1] * latent_here.shape[3], latent_here.shape[-1]
    width = second_here.shape[3]
    for load in loads:
        load.wait()
    out[pl.ds(0, rows), :] = first_here[...].reshape(rows, channels)
    act = norm_silu(latent_here[...].reshape(rows, channels).astype(f32), gain[...][None, :])
    out[pl.ds(rows, rows), :] = act.astype(bf16)
    for r in range(2):
        out[pl.ds(2 * rows + r * width, width), :] = jnp.concatenate([second_here[0, f, r] for f in range(2)], axis=1)


def fetch_kernel(
    packed, first_there, second_here, slots_there, blocks_there, first, second, masks, slots, blocks, sems
):
    del packed
    loads = [
        pltpu.make_async_copy(slots_there, slots, sems.at[0]),
        pltpu.make_async_copy(blocks_there, blocks, sems.at[1]),
        pltpu.make_async_copy(first_there, first, sems.at[2]),
    ]
    for load in loads:
        load.start()
    for load in loads[:2]:
        load.wait()
    me = lax.axis_index("strm")
    for d in range(4):
        for e in range(4):
            chosen = (slots[me ^ d] == me ^ e) & (blocks[me ^ d] > 0)
            masks[d, e] = jnp.full(masks.shape[2:], jnp.where(chosen, 1.0, 0.0), f32)
    taps, group, channels = 27, second_here.shape[-2], second_here.shape[-1]
    values = second_here[...].reshape(taps * group, channels)
    most = (taps + 1) // 2 * group
    second[pl.ds(0, taps * group), :] = values[:, :128]
    right = jnp.concatenate([values[most:, 128:], values[:group, 128:]], axis=0)
    second[pl.ds(taps * group, most), :] = jnp.concatenate([values[:most, 128:], right], axis=1)
    loads[2].wait()


def first_kernel(frames, columns, p0, p1, p2, p3, weight, masks, one, other, two, own, mid):
    packs = (p0, p1, p2, p3)
    upper = lax.axis_index("strm") // 2 == 0
    channels = p0.shape[-1]
    outputs = weight.shape[-2]
    half = frames * columns
    width = 2 * columns

    def chosen(d, at):
        return sum(jnp.where(masks[d, e] > 0.5, packs[e][at, :].astype(f32), 0.0) for e in range(4))

    parts = []
    for d in range(4):
        parts.append(chosen(d, pl.ds(0, half)))
        parts.append(packs[d][pl.ds(half, half), :].astype(f32))
    views = [
        view.astype(bf16).reshape(4, frames + 2, columns, channels)
        for view in shifted(jnp.concatenate(parts, axis=0), columns)
    ]
    rows = 4 * half
    turned = jnp.zeros((3 * outputs, rows), f32)
    taps = [jnp.where(upper, 2, 0), 1, jnp.where(upper, 0, 2)]
    for i in range(3):
        window = jnp.concatenate([view[:, i : i + frames].reshape(rows, channels) for view in views], axis=1)
        kernel = jnp.concatenate(
            [jnp.concatenate([weight[i, taps[j], l] for l in range(3)], axis=1) for j in range(3)], axis=0
        )
        turned = turned + dot(kernel, window, True)

    sums = [turned[j * outputs : (j + 1) * outputs].T for j in range(3)]
    u, v, w = [[halves(values[: 2 * half]), halves(values[2 * half :])] for values in sums]
    far_first = sends_far_first()
    cached = chosen(0, pl.ds(2 * half, 2 * width))
    mid[...] = cached.astype(bf16)
    edges = [cached[:width], cached[width:]]
    far = u + v + [jnp.where(upper, edges[0], edges[1])]
    near = w + [jnp.zeros_like(w[0])] * 2 + [jnp.where(upper, edges[1], edges[0])]
    for n in range(5):
        at = pl.ds(n * half, half)
        one[at, :] = jnp.where(far_first, far[n], near[n]).astype(bf16)
        other[at, :] = jnp.where(far_first, near[n], far[n]).astype(bf16)
    for p in range(2):
        two[pl.ds(p * half, half), :] = u[p].astype(bf16)
        own[pl.ds(p * half, half), :] = v[p]
        own[pl.ds((2 + p) * half, half), :] = w[p]


def sends_far_first():
    return (lax.axis_index("strm") // 2 == 0) == (lax.axis_index("band") % 2 == 0)


def far_comes_first():
    return (lax.axis_index("strm") // 2 == 0) == (lax.axis_index("band") % 2 == 1)


def at_end():
    place = lax.axis_index("band")
    return (place == 0) | (place == lax.axis_size("band") - 1)


def sum_kernel(half, own, one, other, two, *pieces):
    me, place, bands = lax.axis_index("strm"), lax.axis_index("band"), lax.axis_size("band")
    upper = me // 2 == 0
    outside = jnp.where(upper, place == bands - 1, place == 0)
    beyond = jnp.where(upper, place >= bands - 2, place <= 1)
    far_first = far_comes_first()
    alone = at_end()
    channels = pieces[0].shape[-1] // 2
    for p in range(2):
        at = pl.ds(p * half, half)
        after = pl.ds((2 + p) * half, half)
        centre = own[at, :] + other[at, :].astype(f32) + jnp.where(alone, 0.0, one[at, :].astype(f32))
        extra = jnp.where(far_first, jnp.where(alone, 0.0, one[after, :].astype(f32)), other[after, :].astype(f32))
        extra = own[after, :] + extra + jnp.where(beyond, 0.0, two[at, :].astype(f32))
        extra = jnp.where(outside, 0.0, extra)
        for side in range(2):
            lanes = slice(side * channels, (side + 1) * channels)
            both = jnp.concatenate([centre[:, lanes], extra[:, lanes]], axis=1)
            pieces[2 * p + side][...] = both.astype(bf16)


def view_kernel(columns, mid, one, other, views):
    upper = lax.axis_index("strm") // 2 == 0
    far_first = far_comes_first()
    width = 2 * columns
    first_edge = jnp.where(at_end(), 0.0, one[pl.ds(4 * width, width), :].astype(f32))
    second_edge = other[pl.ds(4 * width, width), :].astype(f32)
    far = jnp.where(far_first, first_edge, second_edge)
    near = jnp.where(far_first, second_edge, first_edge)
    top = jnp.where(upper, near, far).astype(bf16)
    bottom = jnp.where(upper, far, near).astype(bf16)
    stored = jnp.concatenate([top, mid[...], bottom], axis=0)
    size = stored.shape[0]
    row = lax.broadcasted_iota(jnp.int32, (size, size), 0)
    column = lax.broadcasted_iota(jnp.int32, (size, size), 1)
    inside = row % width
    natural = 2 * (inside % columns) + inside // columns
    for l in range(3):
        source = natural + (l - 1)
        keep = (source >= 0) & (source < width) & (column == row - inside + source)
        views[l] = dot(jnp.where(keep, 1.0, 0.0).astype(bf16), stored).astype(bf16)


def cache_kernel(columns, views, w0, w1, w2, w3, sums, weights, first_taps):
    me = lax.axis_index("strm")
    channels = sums.shape[-1]
    group = channels // 4
    width = 2 * columns
    area = 2 * width
    for d, quarter in enumerate((w0, w1, w2, w3)):
        at = pl.ds(pl.multiple_of((me ^ d) * group, 16), group)
        first_taps[:, at, pl.ds(0, 128)] = quarter[pl.ds(0, 9 * group), :].reshape(9, group, 128)
        weights[:, at, pl.ds(0, 128)] = quarter[pl.ds(9 * group, 18 * group), :].reshape(18, group, 128)
        others = quarter[pl.ds(27 * group, 14 * group), :].reshape(14, group, 128)
        first_taps[:, at, pl.ds(128, 64)] = others[:9, :, :64]
        weights[pl.ds(0, 5), at, pl.ds(128, 64)] = others[9:, :, :64]
        weights[pl.ds(5, 13), at, pl.ds(128, 64)] = others[:13, :, 64:]

    both = jnp.zeros((2 * area, channels), f32)
    early = jnp.zeros((area, channels), f32)
    for l in range(3):
        c0, c1 = views[l, :, :channels], views[l, :, channels:]
        for j in range(3):
            at = slice(j * width, j * width + area)
            tap = 3 * j + l
            both = both + dot(jnp.concatenate([c0[at], c1[at]], axis=0), first_taps[tap], True)
            early = early + dot(c1[at], weights[tap], True)
    sums[0] = both[:area] + early
    sums[1] = both[area:]


def second_kernel(frames, columns, p0, p1, p2, p3, sums, weights, gain, out, quarters):
    me = lax.axis_index("strm")
    channels = out.shape[-1]
    width = 2 * columns
    for e, piece in enumerate((p0, p1, p2, p3)):
        quarters[me ^ e, 0] = piece[:, :channels]
        quarters[me ^ e, 1] = piece[:, channels:]

    fields = [quarters[q].astype(f32).reshape(2, frames, columns, channels) for q in range(4)]
    row_of = ((1, 1), (0, 0), (1, 0), (0, 1))
    upsampled = jnp.stack(
        [jnp.stack([jnp.stack([fields[2 * a + b][c, t] for b in range(2)]) for a, c in row_of]) for t in range(frames)]
    )
    act = norm_silu(upsampled.reshape(-1, channels), gain[...][None, :])
    left, same, right = [
        v.astype(bf16).reshape(frames, 4, 2, columns, channels) for v in shifted(act, columns)
    ]

    def split(first, second):
        return jnp.stack([first, second], axis=2)

    views = [
        split(left[:, :, 1], same[:, :, 0]),
        same,
        split(same[:, :, 1], right[:, :, 0]),
    ]
    area = 2 * width
    both = sums[...].reshape(2 * area, channels)
    late = jnp.zeros((area, channels), f32)
    for j in range(3):
        for l in range(3):
            window = views[l][:, j : j + 2].reshape(2 * area, channels)
            tap = 3 * j + l
            both = both + dot(window, weights[9 + tap], True)
            late = late + dot(window[:area], weights[tap], True)

    row = lax.broadcasted_iota(jnp.int32, (area, area), 0)
    column = lax.broadcasted_iota(jnp.int32, (area, area), 1)
    inside = row % width
    keep = column == row - inside + (inside % 2) * columns + inside // 2
    order = jnp.where(keep, 1.0, 0.0).astype(bf16)
    for t, branch in enumerate((both[:area], both[area:] + late)):
        base = upsampled[t, 1:3].reshape(area, channels)
        decoded = (base + branch.astype(bf16).astype(f32)).astype(bf16)
        out[0, t] = dot(order, decoded).astype(bf16).reshape(2, width, channels)


def whole(count):
    return [pl.BlockSpec(memory_space=pltpu.VMEM)] * count


THERE = pl.BlockSpec(memory_space=pltpu.HBM)


def there(value):
    return pltpu.with_memory_space_constraint(value, pltpu.HBM)


def call(kernel, name, megabytes, microseconds=1, **settings):
    cost = pl.CostEstimate(flops=int(microseconds * 1e9), bytes_accessed=0, transcendentals=0)
    return pl.pallas_call(
        kernel, name=name, cost_estimate=cost, compiler_params=pltpu.CompilerParams(vmem_limit_bytes=megabytes * 2**20), **settings
    )


def struct(shape, dtype=bf16):
    return jax.ShapeDtypeStruct(shape, dtype)


def body(latents, cache_first, cache_second, gain_first, gain_second, w_first, w_second, cache_slot, block_index):
    frames, columns, channels = latents.shape[1], latents.shape[3], latents.shape[4]
    outputs = w_first.shape[-1]
    bands = lax.axis_size("band")
    streams = lax.axis_size("strm")
    assert outputs == 192 and streams == 4 and bands % 2 == 0 and latents.shape[2] == 1 and frames == 2
    half = frames * columns
    width = 2 * columns

    def swapped(value, distance):
        return lax.ppermute(value, "strm", [(i, i ^ distance) for i in range(streams)])

    def along(value, target):
        pairs = []
        for band in range(bands):
            for k in range(streams):
                to, there = target(band, k)
                if 0 <= to < bands:
                    pairs.append((band * streams + k, to * streams + there))
        return lax.ppermute(value, ("band", "strm"), pairs)

    def first_way(band, k):
        return band ^ 1, k

    def second_way(band, k):
        if band in (0, bands - 1):
            return band, k ^ 1
        return ((band + 1) ^ 1) - 1, k

    def third_way(band, k):
        if bands == 4:
            return band ^ 2, k
        return (band - 2 if k // 2 == 0 else band + 2), k

    turned_first = jnp.swapaxes(w_first, 3, 4)
    turned_second = jnp.swapaxes(w_second, 3, 4)
    group = turned_second.shape[3]
    packed = call(
        pack_kernel,
        "pack",
        4,
        5,
        out_shape=struct((2 * half + 2 * width, channels)),
        in_specs=[THERE] * 4,
        out_specs=whole(1)[0],
        scratch_shapes=[
            pltpu.VMEM(latents.shape, bf16),
            pltpu.VMEM(cache_first.shape, bf16),
            pltpu.VMEM(cache_second.shape, bf16),
            pltpu.VMEM(gain_first.shape, f32),
            pltpu.SemaphoreType.DMA((4,)),
        ],
    )(*map(there, (latents, cache_first, cache_second, gain_first)))
    across = swapped(packed, 2)
    weight_first, weight_own, masks = call(
        fetch_kernel,
        "fetch",
        16,
        0.05,
        out_shape=[struct(turned_first.shape), struct((41 * group, 128)), struct((4, 4, 1, channels), f32)],
        in_specs=whole(1) + [THERE] + whole(1) + [THERE] * 2,
        out_specs=whole(3),
        scratch_shapes=[
            pltpu.SMEM(cache_slot.shape, jnp.int32),
            pltpu.SMEM(block_index.shape, jnp.int32),
            pltpu.SemaphoreType.DMA((3,)),
        ],
    )(packed, there(turned_first), turned_second, there(cache_slot), there(block_index))
    weight_first, across = lax.optimization_barrier((weight_first, across))
    packs = [packed, swapped(packed, 1), across, swapped(across, 1)]
    weights = [weight_own, swapped(weight_own, 1), swapped(weight_own, 2)]
    pair = struct((2 * half, 2 * outputs))
    payload = struct((4 * half + width, 2 * outputs))
    one, other, two, own, mid = call(
        functools.partial(first_kernel, frames, columns),
        "first_conv",
        16,
        1.5,
        out_shape=[payload, payload, pair, struct((4 * half, 2 * outputs), f32), struct((2 * width, 2 * outputs))],
        in_specs=whole(6),
        out_specs=whole(5),
    )(*packs, weight_first, masks)
    one, other, two = along(one, second_way), along(other, first_way), along(two, third_way)
    pieces = call(
        functools.partial(sum_kernel, half),
        "row_sums",
        4,
        1,
        out_shape=[struct((half, 2 * outputs))] * 4,
        in_specs=whole(4),
        out_specs=whole(4),
    )(own, one, other, two)
    across, beyond = swapped(pieces[2], 2), swapped(pieces[3], 3)
    mid, one, other, _ = lax.optimization_barrier((mid, one, other, pieces[0]))
    views = call(
        functools.partial(view_kernel, columns),
        "cached_views",
        4,
        0.1,
        out_shape=struct((3, 4 * width, 2 * outputs)),
        in_specs=whole(3),
        out_specs=whole(1)[0],
    )(mid, one, other)
    weight_across, views = lax.optimization_barrier((weights[2], views))
    weights.append(swapped(weight_across, 1))
    sums, taps = call(
        functools.partial(cache_kernel, columns),
        "cached_conv",
        16,
        1,
        out_shape=[struct((2, 2 * width, outputs), f32), struct((18, outputs, outputs))],
        in_specs=whole(5),
        out_specs=whole(2),
        scratch_shapes=[pltpu.VMEM((9, outputs, outputs), bf16)],
    )(views, *weights)
    beside, _ = lax.optimization_barrier((pieces[1], views))
    pieces = [pieces[0], swapped(beside, 1), across, beyond]
    return call(
        functools.partial(second_kernel, frames, columns),
        "second_conv",
        16,
        out_shape=struct((1, frames, 2, width, outputs)),
        in_specs=whole(7),
        out_specs=whole(1)[0],
        scratch_shapes=[pltpu.VMEM((4, 2, half, outputs), bf16)],
    )(*pieces, sums, taps, gain_second)


def solution(mesh):
    in_specs = (
        P(("grp", "strm"), None, "band", None, None),
        P(("grp", "strm"), None, "band", None, None),
        P(("grp", "strm"), None, "band", None, None),
        P(),
        P(),
        P(None, None, None, None, "strm"),
        P(None, None, None, None, "strm"),
        P("grp"),
        P("grp"),
    )
    out_specs = P(("grp", "strm"), None, "band", None, None)
    return jax.shard_map(body, mesh=mesh, in_specs=in_specs, out_specs=out_specs, check_vma=False)
```

```python
import functools

import jax
import jax.numpy as jnp
from jax import lax
from jax.experimental import pallas as pl
from jax.experimental.pallas import tpu as pltpu
from jax.sharding import PartitionSpec as P

epsilon = 1e-06
f32 = jnp.float32
bf16 = jnp.bfloat16


def norm_silu(values, gain):
    mean_square = jnp.mean(values * values, axis=-1, keepdims=True)
    return jax.nn.silu(values * lax.rsqrt(mean_square + epsilon) * gain)


def dot(lhs, rhs, transposed=False):
    dims = (((1,), (1,)), ((), ())) if transposed else (((1,), (0,)), ((), ()))
    return lax.dot_general(lhs, rhs, dims, preferred_element_type=f32)


def shifted(values, width):
    count = values.shape[0]
    place = lax.broadcasted_iota(jnp.int32, values.shape, 0) % width
    left = jnp.where(place == 0, 0.0, pltpu.roll(values, 1, 0))
    right = jnp.where(place == width - 1, 0.0, pltpu.roll(values, count - 1, 0))
    return left, values, right


def halves(values):
    count = values.shape[0] // 2
    return jnp.concatenate([values[:count], values[count:]], axis=1)


def pack_kernel(latents, first, second, gain_there, out, latent_here, first_here, second_here, gain, sems):
    loads = [
        pltpu.make_async_copy(*pair, sems.at[n])
        for n, pair in enumerate(((gain_there, gain), (latents, latent_here), (first, first_here), (second, second_here)))
    ]
    for load in loads:
        load.start()
    rows, channels = latent_here.shape[1] * latent_here.shape[3], latent_here.shape[-1]
    width = second_here.shape[3]
    for load in loads:
        load.wait()
    out[pl.ds(0, rows), :] = first_here[...].reshape(rows, channels)
    act = norm_silu(latent_here[...].reshape(rows, channels).astype(f32), gain[...][None, :])
    out[pl.ds(rows, rows), :] = act.astype(bf16)
    for r in range(2):
        out[pl.ds(2 * rows + r * width, width), :] = jnp.concatenate([second_here[0, f, r] for f in range(2)], axis=1)


def fetch_kernel(
    packed, first_there, second_here, slots_there, blocks_there, first, second, masks, slots, blocks, sems
):
    del packed
    loads = [
        pltpu.make_async_copy(first_there, first, sems.at[2]),
        pltpu.make_async_copy(slots_there, slots, sems.at[0]),
        pltpu.make_async_copy(blocks_there, blocks, sems.at[1]),
    ]
    for load in loads:
        load.start()
    for load in loads[1:]:
        load.wait()
    me = lax.axis_index("strm")
    for d in range(4):
        for e in range(4):
            chosen = (slots[me ^ d] == me ^ e) & (blocks[me ^ d] > 0)
            masks[d, e] = jnp.full(masks.shape[2:], jnp.where(chosen, 1.0, 0.0), f32)
    taps, group, channels = 27, second_here.shape[-2], second_here.shape[-1]
    values = second_here[...].reshape(taps * group, channels)
    most = (taps + 1) // 2 * group
    second[pl.ds(0, taps * group), :] = values[:, :128]
    right = jnp.concatenate([values[most:, 128:], values[:group, 128:]], axis=0)
    second[pl.ds(taps * group, most), :] = jnp.concatenate([values[:most, 128:], right], axis=1)
    loads[0].wait()


def first_kernel(frames, columns, p0, p1, p2, p3, weight, masks, one, other, two, own, mid):
    packs = (p0, p1, p2, p3)
    upper = lax.axis_index("strm") // 2 == 0
    channels = p0.shape[-1]
    outputs = weight.shape[-2]
    half = frames * columns
    width = 2 * columns

    def chosen(d, at):
        return sum(jnp.where(masks[d, e] > 0.5, packs[e][at, :].astype(f32), 0.0) for e in range(4))

    parts = []
    for d in range(4):
        parts.append(chosen(d, pl.ds(0, half)))
        parts.append(packs[d][pl.ds(half, half), :].astype(f32))
    views = [
        view.astype(bf16).reshape(4, frames + 2, columns, channels)
        for view in shifted(jnp.concatenate(parts, axis=0), columns)
    ]
    rows = 4 * half
    turned = jnp.zeros((3 * outputs, rows), f32)
    taps = [jnp.where(upper, 2, 0), 1, jnp.where(upper, 0, 2)]
    for i in range(3):
        window = jnp.concatenate([view[:, i : i + frames].reshape(rows, channels) for view in views], axis=1)
        kernel = jnp.concatenate(
            [jnp.concatenate([weight[i, taps[j], l] for l in range(3)], axis=1) for j in range(3)], axis=0
        )
        turned = turned + dot(kernel, window, True)

    sums = [turned[j * outputs : (j + 1) * outputs].T for j in range(3)]
    u, v, w = [[halves(values[: 2 * half]), halves(values[2 * half :])] for values in sums]
    far_first = sends_far_first()
    cached = chosen(0, pl.ds(2 * half, 2 * width))
    mid[...] = cached.astype(bf16)
    edges = [cached[:width], cached[width:]]
    far = u + v + [jnp.where(upper, edges[0], edges[1])]
    near = w + [jnp.zeros_like(w[0])] * 2 + [jnp.where(upper, edges[1], edges[0])]
    for n in range(5):
        at = pl.ds(n * half, half)
        one[at, :] = jnp.where(far_first, far[n], near[n]).astype(bf16)
        other[at, :] = jnp.where(far_first, near[n], far[n]).astype(bf16)
    for p in range(2):
        two[pl.ds(p * half, half), :] = u[p].astype(bf16)
        own[pl.ds(p * half, half), :] = v[p]
        own[pl.ds((2 + p) * half, half), :] = w[p]


def sends_far_first():
    return (lax.axis_index("strm") // 2 == 0) == (lax.axis_index("band") % 2 == 0)


def far_comes_first():
    return (lax.axis_index("strm") // 2 == 0) == (lax.axis_index("band") % 2 == 1)


def at_end():
    place = lax.axis_index("band")
    return (place == 0) | (place == lax.axis_size("band") - 1)


def sum_kernel(half, own, one, other, two, *pieces):
    me, place, bands = lax.axis_index("strm"), lax.axis_index("band"), lax.axis_size("band")
    upper = me // 2 == 0
    outside = jnp.where(upper, place == bands - 1, place == 0)
    beyond = jnp.where(upper, place >= bands - 2, place <= 1)
    far_first = far_comes_first()
    alone = at_end()
    channels = pieces[0].shape[-1] // 2
    for p in range(2):
        at = pl.ds(p * half, half)
        after = pl.ds((2 + p) * half, half)
        centre = own[at, :] + other[at, :].astype(f32) + jnp.where(alone, 0.0, one[at, :].astype(f32))
        extra = jnp.where(far_first, jnp.where(alone, 0.0, one[after, :].astype(f32)), other[after, :].astype(f32))
        extra = own[after, :] + extra + jnp.where(beyond, 0.0, two[at, :].astype(f32))
        extra = jnp.where(outside, 0.0, extra)
        for side in range(2):
            lanes = slice(side * channels, (side + 1) * channels)
            both = jnp.concatenate([centre[:, lanes], extra[:, lanes]], axis=1)
            pieces[2 * p + side][...] = both.astype(bf16)


def view_kernel(columns, mid, one, other, views):
    upper = lax.axis_index("strm") // 2 == 0
    far_first = far_comes_first()
    width = 2 * columns
    first_edge = jnp.where(at_end(), 0.0, one[pl.ds(4 * width, width), :].astype(f32))
    second_edge = other[pl.ds(4 * width, width), :].astype(f32)
    far = jnp.where(far_first, first_edge, second_edge)
    near = jnp.where(far_first, second_edge, first_edge)
    top = jnp.where(upper, near, far).astype(bf16)
    bottom = jnp.where(upper, far, near).astype(bf16)
    stored = jnp.concatenate([top, mid[...], bottom], axis=0)
    size = stored.shape[0]
    row = lax.broadcasted_iota(jnp.int32, (size, size), 0)
    column = lax.broadcasted_iota(jnp.int32, (size, size), 1)
    inside = row % width
    natural = 2 * (inside % columns) + inside // columns
    for l in range(3):
        source = natural + (l - 1)
        keep = (source >= 0) & (source < width) & (column == row - inside + source)
        views[l] = dot(jnp.where(keep, 1.0, 0.0).astype(bf16), stored).astype(bf16)


def cache_kernel(columns, views, w0, w1, w2, w3, sums, weights, first_taps):
    me = lax.axis_index("strm")
    channels = sums.shape[-1]
    group = channels // 4
    width = 2 * columns
    area = 2 * width
    for d, quarter in enumerate((w0, w1, w2, w3)):
        at = pl.ds(pl.multiple_of((me ^ d) * group, 16), group)
        first_taps[:, at, pl.ds(0, 128)] = quarter[pl.ds(0, 9 * group), :].reshape(9, group, 128)
        weights[:, at, pl.ds(0, 128)] = quarter[pl.ds(9 * group, 18 * group), :].reshape(18, group, 128)
        others = quarter[pl.ds(27 * group, 14 * group), :].reshape(14, group, 128)
        first_taps[:, at, pl.ds(128, 64)] = others[:9, :, :64]
        weights[pl.ds(0, 5), at, pl.ds(128, 64)] = others[9:, :, :64]
        weights[pl.ds(5, 13), at, pl.ds(128, 64)] = others[:13, :, 64:]

    both = jnp.zeros((2 * area, channels), f32)
    early = jnp.zeros((area, channels), f32)
    for l in range(3):
        c0, c1 = views[l, :, :channels], views[l, :, channels:]
        for j in range(3):
            at = slice(j * width, j * width + area)
            tap = 3 * j + l
            both = both + dot(jnp.concatenate([c0[at], c1[at]], axis=0), first_taps[tap], True)
            early = early + dot(c1[at], weights[tap], True)
    sums[0] = both[:area] + early
    sums[1] = both[area:]


def second_kernel(frames, columns, p0, p1, p2, p3, sums, weights, gain, out, quarters):
    me = lax.axis_index("strm")
    channels = out.shape[-1]
    width = 2 * columns
    for e, piece in enumerate((p0, p1, p2, p3)):
        quarters[me ^ e, 0] = piece[:, :channels]
        quarters[me ^ e, 1] = piece[:, channels:]

    fields = [quarters[q].astype(f32).reshape(2, frames, columns, channels) for q in range(4)]
    row_of = ((1, 1), (0, 0), (1, 0), (0, 1))
    upsampled = jnp.stack(
        [jnp.stack([jnp.stack([fields[2 * a + b][c, t] for b in range(2)]) for a, c in row_of]) for t in range(frames)]
    )
    act = norm_silu(upsampled.reshape(-1, channels), gain[...][None, :])
    left, same, right = [
        v.astype(bf16).reshape(frames, 4, 2, columns, channels) for v in shifted(act, columns)
    ]

    def split(first, second):
        return jnp.stack([first, second], axis=2)

    views = [
        split(left[:, :, 1], same[:, :, 0]),
        same,
        split(same[:, :, 1], right[:, :, 0]),
    ]
    area = 2 * width
    both = sums[...].reshape(2 * area, channels)
    late = jnp.zeros((area, channels), f32)
    for j in range(3):
        for l in range(3):
            window = views[l][:, j : j + 2].reshape(2 * area, channels)
            tap = 3 * j + l
            both = both + dot(window, weights[9 + tap], True)
            late = late + dot(window[:area], weights[tap], True)

    row = lax.broadcasted_iota(jnp.int32, (area, area), 0)
    column = lax.broadcasted_iota(jnp.int32, (area, area), 1)
    inside = row % width
    keep = column == row - inside + (inside % 2) * columns + inside // 2
    order = jnp.where(keep, 1.0, 0.0).astype(bf16)
    for t, branch in enumerate((both[:area], both[area:] + late)):
        base = upsampled[t, 1:3].reshape(area, channels)
        decoded = (base + branch.astype(bf16).astype(f32)).astype(bf16)
        out[0, t] = dot(order, decoded).astype(bf16).reshape(2, width, channels)


def whole(count):
    return [pl.BlockSpec(memory_space=pltpu.VMEM)] * count


THERE = pl.BlockSpec(memory_space=pltpu.HBM)


def there(value):
    return pltpu.with_memory_space_constraint(value, pltpu.HBM)


def call(kernel, name, megabytes, microseconds=1, **settings):
    cost = pl.CostEstimate(flops=int(microseconds * 1e9), bytes_accessed=0, transcendentals=0)
    return pl.pallas_call(
        kernel, name=name, cost_estimate=cost, compiler_params=pltpu.CompilerParams(vmem_limit_bytes=megabytes * 2**20), **settings
    )


def struct(shape, dtype=bf16):
    return jax.ShapeDtypeStruct(shape, dtype)


def body(latents, cache_first, cache_second, gain_first, gain_second, w_first, w_second, cache_slot, block_index):
    frames, columns, channels = latents.shape[1], latents.shape[3], latents.shape[4]
    outputs = w_first.shape[-1]
    bands = lax.axis_size("band")
    streams = lax.axis_size("strm")
    assert outputs == 192 and streams == 4 and bands % 2 == 0 and latents.shape[2] == 1 and frames == 2
    half = frames * columns
    width = 2 * columns

    def swapped(value, distance):
        return lax.ppermute(value, "strm", [(i, i ^ distance) for i in range(streams)])

    def along(value, target):
        pairs = []
        for band in range(bands):
            for k in range(streams):
                to, there = target(band, k)
                if 0 <= to < bands:
                    pairs.append((band * streams + k, to * streams + there))
        return lax.ppermute(value, ("band", "strm"), pairs)

    def first_way(band, k):
        return band ^ 1, k

    def second_way(band, k):
        if band in (0, bands - 1):
            return band, k ^ 1
        return ((band + 1) ^ 1) - 1, k

    def third_way(band, k):
        if bands == 4:
            return band ^ 2, k
        return (band - 2 if k // 2 == 0 else band + 2), k

    turned_first = jnp.swapaxes(w_first, 3, 4)
    turned_second = jnp.swapaxes(w_second, 3, 4)
    group = turned_second.shape[3]
    packed = call(
        pack_kernel,
        "pack",
        4,
        5,
        out_shape=struct((2 * half + 2 * width, channels)),
        in_specs=[THERE] * 4,
        out_specs=whole(1)[0],
        scratch_shapes=[
            pltpu.VMEM(latents.shape, bf16),
            pltpu.VMEM(cache_first.shape, bf16),
            pltpu.VMEM(cache_second.shape, bf16),
            pltpu.VMEM(gain_first.shape, f32),
            pltpu.SemaphoreType.DMA((4,)),
        ],
    )(*map(there, (latents, cache_first, cache_second, gain_first)))
    across = swapped(packed, 2)
    weight_first, weight_own, masks = call(
        fetch_kernel,
        "fetch",
        16,
        0.05,
        out_shape=[struct(turned_first.shape), struct((41 * group, 128)), struct((4, 4, 1, channels), f32)],
        in_specs=whole(1) + [THERE] + whole(1) + [THERE] * 2,
        out_specs=whole(3),
        scratch_shapes=[
            pltpu.SMEM(cache_slot.shape, jnp.int32),
            pltpu.SMEM(block_index.shape, jnp.int32),
            pltpu.SemaphoreType.DMA((3,)),
        ],
    )(packed, there(turned_first), turned_second, there(cache_slot), there(block_index))
    weight_first, across = lax.optimization_barrier((weight_first, across))
    packs = [packed, swapped(packed, 1), across, swapped(across, 1)]
    weights = [weight_own, swapped(weight_own, 1), swapped(weight_own, 2)]
    pair = struct((2 * half, 2 * outputs))
    payload = struct((4 * half + width, 2 * outputs))
    one, other, two, own, mid = call(
        functools.partial(first_kernel, frames, columns),
        "first_conv",
        16,
        1.5,
        out_shape=[payload, payload, pair, struct((4 * half, 2 * outputs), f32), struct((2 * width, 2 * outputs))],
        in_specs=whole(6),
        out_specs=whole(5),
    )(*packs, weight_first, masks)
    one, other, two = along(one, second_way), along(other, first_way), along(two, third_way)
    pieces = call(
        functools.partial(sum_kernel, half),
        "row_sums",
        4,
        1,
        out_shape=[struct((half, 2 * outputs))] * 4,
        in_specs=whole(4),
        out_specs=whole(4),
    )(own, one, other, two)
    across, beyond = swapped(pieces[2], 2), swapped(pieces[3], 3)
    mid, one, other, _ = lax.optimization_barrier((mid, one, other, pieces[0]))
    views = call(
        functools.partial(view_kernel, columns),
        "cached_views",
        4,
        0.1,
        out_shape=struct((3, 4 * width, 2 * outputs)),
        in_specs=whole(3),
        out_specs=whole(1)[0],
    )(mid, one, other)
    weight_across, views = lax.optimization_barrier((weights[2], views))
    weights.append(swapped(weight_across, 1))
    sums, taps = call(
        functools.partial(cache_kernel, columns),
        "cached_conv",
        16,
        1,
        out_shape=[struct((2, 2 * width, outputs), f32), struct((18, outputs, outputs))],
        in_specs=whole(5),
        out_specs=whole(2),
        scratch_shapes=[pltpu.VMEM((9, outputs, outputs), bf16)],
    )(views, *weights)
    beside, sums = lax.optimization_barrier((pieces[1], sums))
    pieces = [pieces[0], swapped(beside, 1), across, beyond]
    return call(
        functools.partial(second_kernel, frames, columns),
        "second_conv",
        16,
        out_shape=struct((1, frames, 2, width, outputs)),
        in_specs=whole(7),
        out_specs=whole(1)[0],
        scratch_shapes=[pltpu.VMEM((4, 2, half, outputs), bf16)],
    )(*pieces, sums, taps, gain_second)


def solution(mesh):
    in_specs = (
        P(("grp", "strm"), None, "band", None, None),
        P(("grp", "strm"), None, "band", None, None),
        P(("grp", "strm"), None, "band", None, None),
        P(),
        P(),
        P(None, None, None, None, "strm"),
        P(None, None, None, None, "strm"),
        P("grp"),
        P("grp"),
    )
    out_specs = P(("grp", "strm"), None, "band", None, None)
    return jax.shard_map(body, mesh=mesh, in_specs=in_specs, out_specs=out_specs, check_vma=False)
```
